32 devices in a mesh: groups: 2 (over x), gx: 8 (over z, y), gy: 2 (over core).
Axes of the slice: x: 2, y: 2, z: 4, core: 2. Of those that a mesh axis runs over, the one named last changes fastest.
Arguments:
- level_set: float32 [512, 128, 128], P(('groups', 'gx'), 'gy'), parts along dimension 0, may hold values from -5 to 5
- normal_speed: float32 [512, 128, 128], P(('groups', 'gx'), 'gy'), parts along dimension 0, may hold values from -1 to 1
- band_tiles: int32 [32, 8], P(('groups', 'gx'), 'gy'), parts along dimension 0, may hold values from 0 to 1, as said below
Outputs:
- surface: float32 [512, 128, 128], P(('groups', 'gx'), 'gy'), parts along dimension 0
The draws below stay inside these ranges and needn't reach their ends.
There are 2 independent parts, one for each index of `groups`. The reference program is written for one: setup_inputs(seed, part) draws one part's arguments, and reference() takes and returns one part's arrays. A program takes and returns all parts, laid end to end along the dimension named above; each array names one. Nothing has to cross between parts.
Inputs may be any that keep to these rules, and one draw needn't show every extreme that they name: `band_tiles`: in each aligned block of four bricks along gx with the same gy index exactly 12 tiles are band tiles, each aligned pair of bricks in the block holds an even number of them, and one brick of every block has all 8 of its tiles in the band.
All inputs are finite; a program needn't handle non-finite values.
Results may differ from the reference program's by a relative error of at most 0.0003.
Values sent between devices are 32-bit elements; how exact they have to be, the bound alone decides.
A program may use at most 64 MiB of HBM per device.

```python
import jax
import jax.numpy as jnp
from jax import lax

CX = 32
TILE = 16
BAND = 3
RK_STEPS = 2
REINIT = 12
NX = 256
NY = 128
NZ = 128
TX = 2
TY = 4
SLOTS = 8
NTX = 16
NTY = 8
N_GX = 8
N_GY = 2


def draw_band_tiles(key, part):
    key = jax.random.fold_in(key, 11)
    subkeys = jax.random.split(key, 4)
    blocks = N_GX // 4
    heaviest = jax.random.randint(subkeys[0], (blocks, N_GY, 1), 0, 4)
    paired = 2 * jax.random.randint(subkeys[1], (blocks, N_GY, 1), 0, (4 * BAND - SLOTS) // 2 + 1)
    remainder = 4 * BAND - SLOTS - paired
    split_at = jax.random.randint(subkeys[2], (blocks, N_GY, 1), 0, remainder + 1)
    where_pos = jnp.arange(4, dtype=jnp.int32)[None, None, :]
    loads = jnp.where(where_pos == heaviest, SLOTS, jnp.where(where_pos == jnp.bitwise_xor(heaviest, 1), paired, jnp.where(where_pos == jnp.bitwise_xor(heaviest, 2), split_at, remainder - split_at)))
    loads = jnp.transpose(loads, (0, 2, 1)).reshape(N_GX, N_GY)
    scores = jax.random.randint(subkeys[3], (N_GX, N_GY, SLOTS), 0, 1 << 20) * SLOTS + jnp.arange(SLOTS, dtype=jnp.int32)
    ranking = jnp.argsort(jnp.argsort(scores, axis=-1), axis=-1)
    inband = (ranking < loads[:, :, None]).astype(jnp.int32)
    return inband.reshape(N_GX, N_GY, TX, TY).transpose(0, 2, 1, 3).reshape(NTX, NTY)


def levels(own_key, dims, cuts, low, high):
    factor_of = 1.0
    for dim, shards_of in cuts:
        steps = jax.random.uniform(jax.random.fold_in(jax.random.fold_in(own_key, 6), dim), (shards_of,), jnp.float32, low / len(cuts), high / len(cuts))
        factor_of = factor_of * jnp.repeat(jnp.exp(steps), dims[dim] // shards_of).reshape((-1,) + (1,) * (len(dims) - 1 - dim))
    return factor_of


def centred(rng, shape, width, limit, cuts=(), kind=jnp.bfloat16):
    gain = levels(rng, shape, cuts, -0.22, 0.18) if cuts else 1.0
    entries = jax.random.normal(rng, shape, jnp.float32) * width * gain
    return jnp.minimum(jnp.maximum(entries, -limit), limit).astype(kind)


def setup_inputs(seed: int = 0, part: int = 0) -> dict:
    seeds = jax.random.split(jax.random.key(seed), 4)
    part_keys = jax.random.split(jax.random.fold_in(seeds[3], part), 4)
    level_set = centred(part_keys[0], (NX, NY, NZ), 1.0, 5.0, ((0, 8), (1, 2)), jnp.float32)
    normal_speed = jnp.clip(jax.random.uniform(part_keys[1], (NX, NY, NZ), jnp.float32, -1.0, 1.0) * levels(part_keys[1], (NX, NY, NZ), ((0, 8), (1, 2)), -0.4, 0.0), -1.0, 1.0)
    band_tiles = draw_band_tiles(jax.random.fold_in(jax.random.fold_in(seeds[3], part), 71), part)
    return dict(level_set=level_set, normal_speed=normal_speed, band_tiles=band_tiles)


TIME_STEP = 0.25
REINIT_STEP = 0.3
WENO_EPS = 1e-06

def weno_blend(far_left, near_left, center, near_right, far_right):
    smooth_one = 13.0 / 12.0 * (far_left - 2.0 * near_left + center) ** 2 + 0.25 * (far_left - 4.0 * near_left + 3.0 * center) ** 2
    smooth_two = 13.0 / 12.0 * (near_left - 2.0 * center + near_right) ** 2 + 0.25 * (near_left - near_right) ** 2
    smooth_three = 13.0 / 12.0 * (center - 2.0 * near_right + far_right) ** 2 + 0.25 * (3.0 * center - 4.0 * near_right + far_right) ** 2
    weight_one = 0.1 / (WENO_EPS + smooth_one) ** 2
    weight_two = 0.6 / (WENO_EPS + smooth_two) ** 2
    weight_three = 0.3 / (WENO_EPS + smooth_three) ** 2
    stencil_one = far_left / 3.0 - 7.0 * near_left / 6.0 + 11.0 * center / 6.0
    stencil_two = -near_left / 6.0 + 5.0 * center / 6.0 + near_right / 3.0
    stencil_three = center / 3.0 + 5.0 * near_right / 6.0 - far_right / 6.0
    total = weight_one * stencil_one + weight_two * stencil_two + weight_three * stencil_three
    return total / (weight_one + weight_two + weight_three)

def evolution_rate(padded, velocity):
    extent = velocity.shape
    upwind_pos = jnp.zeros(extent, jnp.float32)
    upwind_neg = jnp.zeros(extent, jnp.float32)
    for direction in range(3):
        cropped = padded
        for crosswise in range(3):
            if crosswise != direction:
                cropped = lax.slice_in_dim(cropped, 3, 3 + extent[crosswise], axis=crosswise)
        length = extent[direction]
        increments = lax.slice_in_dim(cropped, 1, length + 6, axis=direction) - lax.slice_in_dim(cropped, 0, length + 5, axis=direction)
        shifted = [lax.slice_in_dim(increments, offset, offset + length, axis=direction) for offset in range(6)]
        behind = weno_blend(shifted[0], shifted[1], shifted[2], shifted[3], shifted[4])
        forward = weno_blend(shifted[5], shifted[4], shifted[3], shifted[2], shifted[1])
        upwind_pos = upwind_pos + jnp.maximum(jnp.maximum(behind, 0.0) ** 2, jnp.minimum(forward, 0.0) ** 2)
        upwind_neg = upwind_neg + jnp.maximum(jnp.minimum(behind, 0.0) ** 2, jnp.maximum(forward, 0.0) ** 2)
    magnitude = jnp.where(velocity > 0.0, jnp.sqrt(upwind_pos), jnp.sqrt(upwind_neg))
    return velocity * magnitude

def reinitialize(tile_stack):
    start_tiles = tile_stack
    signum = start_tiles / jnp.sqrt(start_tiles * start_tiles + 1.0)

    def one_sweep(iteration, current):
        upwind_pos = jnp.zeros(current.shape, current.dtype)
        upwind_neg = jnp.zeros(current.shape, current.dtype)
        for direction in (1, 2, 3):
            widths = [(0, 0), (0, 0), (0, 0), (0, 0)]
            widths[direction] = (1, 1)
            padded = jnp.pad(current, widths, mode='edge')
            length = current.shape[direction]
            behind = current - lax.slice_in_dim(padded, 0, length, axis=direction)
            forward = lax.slice_in_dim(padded, 2, length + 2, axis=direction) - current
            upwind_pos = upwind_pos + jnp.maximum(jnp.maximum(behind, 0.0) ** 2, jnp.minimum(forward, 0.0) ** 2)
            upwind_neg = upwind_neg + jnp.maximum(jnp.minimum(behind, 0.0) ** 2, jnp.maximum(forward, 0.0) ** 2)
        magnitude = jnp.where(start_tiles > 0.0, jnp.sqrt(upwind_pos), jnp.sqrt(upwind_neg))
        return current - REINIT_STEP * signum * (magnitude - 1.0)
    return lax.fori_loop(0, REINIT, one_sweep, tile_stack)

def reference(level_set, normal_speed, band_tiles):
    block_rows = 4 * CX

    def full_rate(field_now):
        padded = jnp.pad(field_now, 3)

        def one_block(block_index):
            first_row = block_index * block_rows
            segment = lax.dynamic_slice_in_dim(padded, first_row, block_rows + 6, 0)
            velocity = lax.dynamic_slice_in_dim(normal_speed, first_row, block_rows, 0)
            return evolution_rate(segment, velocity)
        blocks = lax.map(one_block, jnp.arange(NX // block_rows, dtype=jnp.int32))
        return blocks.reshape(NX, NY, NZ)
    surface = level_set
    for advance in range(RK_STEPS):
        halfway = surface - TIME_STEP * full_rate(surface)
        surface = 0.5 * surface + 0.5 * (halfway - TIME_STEP * full_rate(halfway))
    tile_view = surface.reshape(NTX, TILE, NTY, TILE, NZ).transpose(0, 2, 1, 3, 4)
    redone = lax.map(reinitialize, tile_view)
    chosen = jnp.where(band_tiles[:, :, None, None, None] > 0, redone, tile_view)
    return chosen.transpose(0, 2, 1, 3, 4).reshape(NX, NY, NZ)
```

```python
import functools

import jax
import jax.numpy as jnp
from jax import lax
from jax.experimental import pallas as pl
from jax.experimental.pallas import tpu as pltpu
from jax.sharding import PartitionSpec as P

TILE = 16
RK_STEPS = 2
REINIT = 12
STAGES = 2 * RK_STEPS
GHOST = 3
SCALE = 1.5 ** 0.5
STEP = 0.125
EPS = 0.75e-6
TINY = 1e-37
PITCH = 144
OUT_PITCH = 136
ZPAD = 8
MESH = pl.DeviceIdType.MESH


def rcp(x):
    return pl.reciprocal(x, approx=True)


def root(x):
    return x * lax.rsqrt(jnp.maximum(x, TINY))


def stencil(x, y):
    e = y - x
    f = e * (1.0 / 3.0)
    mid = (e * f) * 2.0 + ((x * y) * 0.5 + EPS)
    left = mid + y * e
    right = mid - x * e
    rm = rcp(mid)
    rl = rcp(left)
    rr = rcp(right)
    b = (rm * rm) * 6.0
    a = rl * rl
    w = rr * rr
    a3 = a * 3.0
    w3 = w * 3.0
    r1 = y + f
    l1 = x - f
    return (
        (a, a3, a * (r1 + f), a3 * r1),
        (b, b * (y - f), b * (x + f)),
        (w, w3, w * (l1 - f), w3 * l1),
    )


def push(state, phi):
    last_phi, last_d, older_d, last_g, left_old, left_new, mid_new = state
    d = phi - last_phi
    g = d - last_d
    left, mid, right = stencil(last_g, g)
    a, a3, ar2, ar1 = left_old
    b, bc2, bc1 = mid_new
    w, w3, wl2, wl1 = right
    c2 = older_d + older_d
    behind = c2 + (ar2 + bc2 + wl1) * rcp(a + b + w3)
    ahead = (wl2 + bc1 + ar1) * rcp(w + b + a3) - c2
    return (phi, d, last_d, g, left_new, left, mid), behind, ahead


def begin(cells):
    p0, p1, p2, p3, p4 = cells
    d1, d2, d3, d4 = p1 - p0, p2 - p1, p3 - p2, p4 - p3
    g1, g2, g3 = d2 - d1, d3 - d2, d4 - d3
    left_a, _, _ = stencil(g1, g2)
    left_b, mid_b, _ = stencil(g2, g3)
    return (p4, d4, d3, g3, left_a, left_b, mid_b)


def upwind(sign, behind, ahead):
    v = jnp.maximum(jnp.maximum(sign * behind, sign * ahead), 0.0)
    return v * v


def advance_kernel(
    rows, cols, n_gx, n_gy,
    level_ref, speed_hbm, out_ref,
    field, speed, sign, acc_y, acc_z, zin, zout, zsign, yface, yhalo,
    send_sem, recv_sem, local_sem,
):
    cells = rows * cols
    pad = GHOST * cols
    span = cells + 2 * pad
    blocks = cells // 128
    groups = blocks // 8
    gx = lax.axis_index("gx")
    gy = lax.axis_index("gy")
    low_x, high_x = gx > 0, gx < n_gx - 1
    low_y, high_y = gy > 0, gy < n_gy - 1
    sides = (
        (low_x, {"gx": gx - 1}), (high_x, {"gx": gx + 1}),
        (low_y, {"gy": gy - 1}), (high_y, {"gy": gy + 1}),
    )

    load_level = pltpu.make_async_copy(level_ref, acc_y, local_sem.at[0])
    load_speed = pltpu.make_async_copy(speed_hbm, speed, local_sem.at[1])
    load_level.start()
    load_speed.start()

    barrier = pltpu.get_barrier_semaphore()
    for there, device in sides:
        @pl.when(there)
        def _():
            pl.semaphore_signal(barrier, inc=1, device_id=device, device_id_type=MESH)

    zero = jnp.zeros((pad, 128), jnp.float32)
    for stage in range(STAGES):
        @pl.when(jnp.logical_not(low_x))
        def _():
            field[pl.ds(stage * span, pad)] = zero

        @pl.when(jnp.logical_not(high_x))
        def _():
            field[pl.ds(stage * span + pad + cells, pad)] = zero

        @pl.when(jnp.logical_not(low_y))
        def _():
            yhalo[pl.ds((stage * 2) * GHOST * rows, GHOST * rows)] = zero[: GHOST * rows]

        @pl.when(jnp.logical_not(high_y))
        def _():
            yhalo[pl.ds((stage * 2 + 1) * GHOST * rows, GHOST * rows)] = zero[: GHOST * rows]

    for block in range(blocks):
        zin[pl.ds(block * PITCH, ZPAD)] = jnp.zeros((ZPAD, 128), jnp.float32)
        zin[pl.ds(block * PITCH + ZPAD + 128, ZPAD)] = jnp.zeros((ZPAD, 128), jnp.float32)

    load_speed.wait()

    def signs(block, carry):
        at = pl.multiple_of(block * 128, 128)
        v = jnp.where(speed[pl.ds(at, 128)] > 0.0, 1.0, -1.0)
        sign[pl.ds(at, 128)] = v
        zsign[pl.ds(pl.multiple_of(block * OUT_PITCH, 8), 128)] = v.T
        return carry

    lax.fori_loop(0, blocks, signs, 0)
    load_level.wait()

    def scaled(block, carry):
        at = pl.multiple_of(block * 128, 128)
        field[pl.ds(pad + at, 128)] = acc_y[pl.ds(at, 128)] * SCALE
        return carry

    lax.fori_loop(0, blocks, scaled, 0)

    there_count = sum(there.astype(jnp.int32) for there, _ in sides)
    pl.semaphore_wait(barrier, there_count)

    def copies(stage):
        base = stage * span
        face = GHOST * rows
        made = []
        for direction, (src, src_at, dst, dst_at, count) in enumerate((
            (field, base + pad, field, base + pad + cells, pad),
            (field, base + cells, field, base, pad),
            (yface, (stage * 2) * face, yhalo, (stage * 2 + 1) * face, face),
            (yface, (stage * 2 + 1) * face, yhalo, (stage * 2) * face, face),
        )):
            made.append(pltpu.make_async_remote_copy(
                src_ref=src.at[pl.ds(src_at, count)],
                dst_ref=dst.at[pl.ds(dst_at, count)],
                send_sem=send_sem.at[stage * 4 + direction],
                recv_sem=recv_sem.at[stage * 4 + direction],
                device_id=sides[direction][1],
                device_id_type=MESH,
            ))
        return made

    def one_stage(stage, carry):
        base = stage * span
        own = base + pad
        face = GHOST * rows
        sends = copies(stage)
        for direction in (0, 1):
            @pl.when(sides[direction][0])
            def _(direction=direction):
                sends[direction].start()
        for side in range(2):
            for n in range(GHOST):
                y = n if side == 0 else cols - GHOST + n
                for x in range(0, rows, 8):
                    yface[pl.ds((stage * 2 + side) * face + n * rows + x, 8)] = field[
                        pl.ds(own + x * cols + y, 8, stride=cols)
                    ]
        for direction in (2, 3):
            @pl.when(sides[direction][0])
            def _(direction=direction):
                sends[direction].start()

        def flip(block, carry):
            zin[pl.ds(pl.multiple_of(block * PITCH + ZPAD, 8), 128)] = field[
                pl.ds(pl.multiple_of(own + block * 128, 64), 128)
            ].T
            return carry

        lax.fori_loop(0, blocks, flip, 0, unroll=4)

        def z_cell(group, z):
            return zin[pl.ds(group * 8 * PITCH + ZPAD + z, 8, stride=PITCH)]

        depth = 128
        per = 4
        state = tuple(begin([z_cell(q, z) for z in range(-3, 2)]) for q in range(groups))
        firsts = [push(state[q], z_cell(q, 2)) for q in range(groups)]

        def z_steps(index, carry):
            start = index * per
            out = []
            for q in range(groups):
                st, behind = carry[q]
                for u in range(per):
                    z = start + u
                    st, next_behind, ahead = push(st, z_cell(q, z + 3))
                    at = pl.ds(q * 8 * OUT_PITCH + z, 8, stride=OUT_PITCH)
                    zout[at] = upwind(zsign[at], behind, ahead)
                    behind = next_behind
                out.append((st, behind))
            return tuple(out)

        lax.fori_loop(0, depth // per, z_steps, tuple((s, m) for s, m, _ in firsts))

        def unflip(block, carry):
            acc_z[pl.ds(pl.multiple_of(block * 128, 128), 128)] = zout[
                pl.ds(pl.multiple_of(block * OUT_PITCH, 8), 128)
            ].T
            return carry

        lax.fori_loop(0, blocks, unflip, 0, unroll=4)

        for direction, there in ((2, high_y), (3, low_y)):
            @pl.when(there)
            def _(direction=direction):
                sends[direction].wait_recv()

        ways = 2

        def y_block(pair, carry):
            xs = [(pair * ways + q) * 8 for q in range(ways)]

            def low_cell(x, n):
                return yhalo[pl.ds(pl.multiple_of((stage * 2) * face + n * rows + x, 8), 8)]

            def high_cell(x, n):
                return yhalo[pl.ds(pl.multiple_of((stage * 2 + 1) * face + n * rows + x, 8), 8)]

            def cell(x, y):
                return field[pl.ds(own + x * cols + y, 8, stride=cols)]

            def steps(start, count, carry, source):
                out = []
                for q, x in enumerate(xs):
                    st, behind = carry[q]
                    for u in range(count):
                        st, next_behind, ahead = push(st, source(x, u))
                        at = pl.ds(x * cols + start + u, 8, stride=cols)
                        acc_y[at] = upwind(sign[at], behind, ahead)
                        behind = next_behind
                    out.append((st, behind))
                return tuple(out)

            firsts = []
            for x in xs:
                st = begin([low_cell(x, n) for n in range(GHOST)] + [cell(x, 0), cell(x, 1)])
                st, behind, _ = push(st, cell(x, 2))
                firsts.append((st, behind))
            per = 4
            trips = (cols - GHOST) // per
            carry = lax.fori_loop(
                0, trips,
                lambda i, c: steps(i * per, per, c, lambda x, u: cell(x, i * per + u + GHOST)),
                tuple(firsts),
            )
            done = trips * per
            rest = cols - GHOST - done
            if rest:
                carry = steps(done, rest, carry, lambda x, u: cell(x, done + u + GHOST))
            steps(cols - GHOST, GHOST, carry, high_cell)
            return 0

        lax.fori_loop(0, rows // (8 * ways), y_block, 0)

        for direction, there in ((0, high_x), (1, low_x)):
            @pl.when(there)
            def _(direction=direction):
                sends[direction].wait_recv()

        odd = lax.rem(stage, 2) == 1
        last = jnp.where(stage == STAGES - 1, jnp.float32(1.0 / SCALE), jnp.float32(1.0))
        keep = jnp.where(odd, jnp.float32(0.5), jnp.float32(0.0)) * last
        take = jnp.where(odd, jnp.float32(0.5), jnp.float32(1.0)) * last
        before = jnp.maximum(stage - 1, 0) * span + pad
        after = base + span + pad

        def x_block(pair, carry):
            ys = [(pair * ways + q) * 8 for q in range(ways)]

            def cell(y, x):
                return field[pl.ds(pl.multiple_of(own + x * cols + y, 8), 8)]

            firsts = []
            for y in ys:
                st = begin([cell(y, x) for x in range(-3, 2)])
                st, behind, _ = push(st, cell(y, 2))
                firsts.append((st, behind))
            per = 4

            def steps(index, carry):
                out = []
                for q, y in enumerate(ys):
                    st, behind = carry[q]
                    for u in range(per):
                        x = index * per + u
                        st, next_behind, ahead = push(st, cell(y, x + 3))
                        off = pl.multiple_of(x * cols + y, 8)
                        at = pl.ds(off, 8)
                        total = upwind(sign[at], behind, ahead) + (acc_y[at] + acc_z[at])
                        moved = cell(y, x) - (speed[at] * STEP) * root(total)
                        older = field[pl.ds(pl.multiple_of(before + off, 8), 8)]
                        field[pl.ds(pl.multiple_of(after + off, 8), 8)] = keep * older + take * moved
                        behind = next_behind
                    out.append((st, behind))
                return tuple(out)

            lax.fori_loop(0, rows // per, steps, tuple(firsts))
            return 0

        lax.fori_loop(0, cols // (8 * ways), x_block, 0)

        for direction in range(4):
            @pl.when(sides[direction][0])
            def _(direction=direction):
                sends[direction].wait_send()
        return carry

    lax.fori_loop(0, STAGES, one_stage, 0)
    store = pltpu.make_async_copy(
        field.at[pl.ds(STAGES * span + pad, cells)], out_ref, local_sem.at[0]
    )
    store.start()
    store.wait()


def advance(level_set, normal_speed, rows, cols, n_gx, n_gy):
    cells = rows * cols
    blocks = cells // 128
    span = cells + 2 * GHOST * cols
    flat = pltpu.VMEM((cells, 128), jnp.float32)
    return pl.pallas_call(
        functools.partial(advance_kernel, rows, cols, n_gx, n_gy),
        out_shape=jax.ShapeDtypeStruct((cells, 128), jnp.float32),
        in_specs=[pl.BlockSpec(memory_space=pl.ANY)] * 2,
        out_specs=pl.BlockSpec(memory_space=pl.ANY),
        scratch_shapes=[
            pltpu.VMEM(((STAGES + 1) * span, 128), jnp.float32),
            flat, flat, flat, flat,
            pltpu.VMEM((blocks * PITCH, 128), jnp.float32),
            pltpu.VMEM((blocks * OUT_PITCH, 128), jnp.float32),
            pltpu.VMEM((blocks * OUT_PITCH, 128), jnp.float32),
            pltpu.VMEM((STAGES * 2 * GHOST * rows, 128), jnp.float32),
            pltpu.VMEM((STAGES * 2 * GHOST * rows, 128), jnp.float32),
            pltpu.SemaphoreType.DMA((STAGES * 4,)),
            pltpu.SemaphoreType.DMA((STAGES * 4,)),
            pltpu.SemaphoreType.DMA((2,)),
        ],
        compiler_params=pltpu.CompilerParams(
            collective_id=0, has_side_effects=True, vmem_limit_bytes=28 * 2**20
        ),
        name="advance",
    )(level_set, normal_speed)


def reinit_kernel(rows, cols, field, band, out, t, gain, sign):
    wide = cols // TILE
    down = rows // TILE

    def source(i, j, d):
        return pl.ds((d * TILE + i) * cols + j, wide, stride=TILE)

    def gather(i, carry):
        for j in range(TILE):
            v = jnp.concatenate([field[source(i, j, d)] for d in range(down)], axis=0)
            at = pl.ds(pl.multiple_of((i * TILE + j) * 8, 8), 8)
            t[0, at] = v
            gain[at] = (0.3 * v) * lax.rsqrt(v * v + 1.0)
            sign[at] = jnp.where(v > 0.0, 1.0, -1.0)
        return carry

    lax.fori_loop(0, TILE, gather, 0)
    lane = lax.broadcasted_iota(jnp.int32, (8, 128), 1)
    first = lane == 0

    def sweep(index, carry):
        now = lax.rem(index, 2)
        later = 1 - now

        def line(i, carry):
            above = jnp.maximum(i - 1, 0) * TILE
            below = jnp.minimum(i + 1, TILE - 1) * TILE
            here = i * TILE

            def cell(row, j):
                return t[now, pl.ds(pl.multiple_of((row + j) * 8, 8), 8)]

            values = [cell(here, j) for j in range(TILE)]
            for j in range(TILE):
                v = values[j]
                at = pl.ds(pl.multiple_of((here + j) * 8, 8), 8)
                s = sign[at]
                total = None
                mz = jnp.where(first, 0.0, v - pltpu.roll(v, 1, 1))
                pairs = [
                    (v - cell(above, j), v - cell(below, j)),
                    (v - values[max(j - 1, 0)], v - values[min(j + 1, TILE - 1)]),
                    (mz, -pltpu.roll(mz, 127, 1)),
                ]
                for m, nq in pairs:
                    u = jnp.maximum(jnp.maximum(s * m, s * nq), 0.0)
                    total = u * u if total is None else total + u * u
                t[later, at] = v - gain[at] * (root(total) - 1.0)
            return carry

        lax.fori_loop(0, TILE, line, 0)
        return carry

    lax.fori_loop(0, REINIT, sweep, 0)
    final = REINIT % 2

    def scatter(i, carry):
        for j in range(TILE):
            v = t[final, pl.ds(pl.multiple_of((i * TILE + j) * 8, 8), 8)]
            for d in range(down):
                at = source(i, j, d)
                mask = band[pl.ds(d * wide, wide)]
                out[at] = jnp.where(mask > 0, v[d * wide : (d + 1) * wide], field[at])
        return carry

    lax.fori_loop(0, TILE, scatter, 0)


def reinitialize(field, band, rows, cols):
    cells = rows * cols
    flat = pltpu.VMEM((cells, 128), jnp.float32)
    return pl.pallas_call(
        functools.partial(reinit_kernel, rows, cols),
        out_shape=jax.ShapeDtypeStruct((cells, 128), jnp.float32),
        in_specs=[pl.BlockSpec(memory_space=pltpu.VMEM)] * 2,
        out_specs=pl.BlockSpec(memory_space=pltpu.VMEM),
        scratch_shapes=[pltpu.VMEM((2, cells, 128), jnp.float32), flat, flat],
        compiler_params=pltpu.CompilerParams(vmem_limit_bytes=24 * 2**20),
        name="reinitialize",
    )(field, band)


def solution(mesh):
    n_gx, n_gy = mesh.shape["gx"], mesh.shape["gy"]

    def body(level_set, normal_speed, band_tiles):
        rows, cols, depth = level_set.shape
        cells = rows * cols
        field = advance(
            level_set.reshape(cells, depth), normal_speed.reshape(cells, depth),
            rows, cols, n_gx, n_gy,
        )
        band = jnp.broadcast_to(band_tiles.reshape(-1, 1), (band_tiles.size, 128))
        return reinitialize(field, band, rows, cols).reshape(rows, cols, depth)

    return jax.shard_map(
        body,
        mesh=mesh,
        in_specs=(
            P(("groups", "gx"), "gy", None),
            P(("groups", "gx"), "gy", None),
            P(("groups", "gx"), "gy"),
        ),
        out_specs=P(("groups", "gx"), "gy", None),
        check_vma=False,
    )
```

```python
import functools

import jax
import jax.numpy as jnp
from jax import lax
from jax.experimental import pallas as pl
from jax.experimental.pallas import tpu as pltpu
from jax.sharding import PartitionSpec as P

TILE = 16
RK_STEPS = 2
REINIT = 12
STAGES = 2 * RK_STEPS
GHOST = 3
SCALE = 1.5 ** 0.5
STEP = 0.125
EPS = 0.75e-6
TINY = 1e-37
PITCH = 140
OUT_PITCH = 132
ZPAD = 4
GAP = 8
UNROLL = 16
PARTS = 4
MESH = pl.DeviceIdType.MESH


def rcp(x):
    return pl.reciprocal(x, approx=True)


def root(x):
    return x * lax.rsqrt(jnp.maximum(x, TINY))


def stencil(x, y):
    e = y - x
    f = e * (1.0 / 3.0)
    mid = (e * f) * 2.0 + ((x * y) * 0.5 + EPS)
    left = mid + y * e
    right = mid - x * e
    rm = rcp(mid)
    rl = rcp(left)
    rr = rcp(right)
    b = (rm * rm) * 6.0
    a = rl * rl
    w = rr * rr
    a3 = a * 3.0
    w3 = w * 3.0
    r1 = y + f
    l1 = x - f
    return (
        (a, a3, a * (r1 + f), a3 * r1),
        (b, b * (y - f), b * (x + f)),
        (w, w3, w * (l1 - f), w3 * l1),
    )


def push(state, phi):
    last_phi, last_d, older_d, last_g, left_old, left_new, mid_new = state
    d = phi - last_phi
    g = d - last_d
    left, mid, right = stencil(last_g, g)
    a, a3, ar2, ar1 = left_old
    b, bc2, bc1 = mid_new
    w, w3, wl2, wl1 = right
    c2 = older_d + older_d
    behind = c2 + (ar2 + bc2 + wl1) * rcp(a + b + w3)
    ahead = (wl2 + bc1 + ar1) * rcp(w + b + a3) - c2
    return (phi, d, last_d, g, left_new, left, mid), behind, ahead


def begin(cells):
    p0, p1, p2, p3, p4 = cells
    d1, d2, d3, d4 = p1 - p0, p2 - p1, p3 - p2, p4 - p3
    g1, g2, g3 = d2 - d1, d3 - d2, d4 - d3
    left_a, _, _ = stencil(g1, g2)
    left_b, mid_b, _ = stencil(g2, g3)
    return (p4, d4, d3, g3, left_a, left_b, mid_b)


def upwind(sign, behind, ahead):
    v = jnp.maximum(jnp.maximum(sign * behind, sign * ahead), 0.0)
    return v * v


def advance_kernel(
    rows, cols, n_gx, n_gy,
    level_hbm, speed_hbm, out_ref,
    field_a, field_b, speed, sign, acc_y, acc_z, zin, zout, zsign, yface, yhalo,
    send_sem, recv_sem, local_sem, store_sem,
):
    cells = rows * cols
    pitch = cols + GAP
    own = GHOST * pitch
    blocks = cells // 128
    block_rows = 128 // cols
    groups = blocks // 8
    face = GHOST * rows
    gx = lax.axis_index("gx")
    gy = lax.axis_index("gy")
    low_x, high_x = gx > 0, gx < n_gx - 1
    low_y, high_y = gy > 0, gy < n_gy - 1
    sides = (
        (low_x, {"gx": gx - 1}), (high_x, {"gx": gx + 1}),
        (low_y, {"gy": gy - 1}), (high_y, {"gy": gy + 1}),
    )

    part = cells // PARTS
    loads = []
    for n in range(PARTS):
        at = pl.ds(n * part, part)
        loads.append((
            pltpu.make_async_copy(level_hbm.at[at], acc_z.at[at], local_sem.at[n]),
            pltpu.make_async_copy(speed_hbm.at[at], speed.at[at], local_sem.at[PARTS + n]),
        ))
    for level, _ in loads:
        level.start()
    for _, rate in loads:
        rate.start()

    barrier = pltpu.get_barrier_semaphore()
    for there, device in sides:
        @pl.when(there)
        def _():
            pl.semaphore_signal(barrier, inc=1, device_id=device, device_id_type=MESH)

    zero = jnp.zeros((own, 128), jnp.float32)
    gap = jnp.zeros((GAP, 128), jnp.float32)
    for field in (field_a, field_b):
        for x in range(rows):
            field[pl.ds(own + x * pitch + cols, GAP)] = gap

        @pl.when(jnp.logical_not(low_x))
        def _():
            field[pl.ds(0, own)] = zero

        @pl.when(jnp.logical_not(high_x))
        def _():
            field[pl.ds(own + rows * pitch, own)] = zero

    for stage in range(STAGES):
        @pl.when(jnp.logical_not(low_y))
        def _():
            yhalo[pl.ds((stage * 2) * face, face)] = zero[:face]

        @pl.when(jnp.logical_not(high_y))
        def _():
            yhalo[pl.ds((stage * 2 + 1) * face, face)] = zero[:face]

    for block in range(blocks):
        zin[pl.ds(block * PITCH, ZPAD)] = gap[:ZPAD]
        zin[pl.ds(block * PITCH + ZPAD + 128, PITCH - 128 - ZPAD)] = gap[: PITCH - 128 - ZPAD]

    def natural(x, y):
        return pl.ds(pl.multiple_of(x * cols + y, 8), 8)

    def spaced(x, y):
        return pl.ds(pl.multiple_of(x * pitch + y, 8), 8)

    for level, _ in loads:
        level.wait()

    def scaled(x, carry):
        field_a[pl.ds(pl.multiple_of(own + x * pitch, 8), cols)] = (
            acc_z[pl.ds(pl.multiple_of(x * cols, 8), cols)] * SCALE
        )
        return carry

    lax.fori_loop(0, rows, scaled, 0)
    for _, rate in loads:
        rate.wait()

    def signs(block, carry):
        v = jnp.where(speed[pl.ds(pl.multiple_of(block * 128, 128), 128)] > 0.0, 1.0, -1.0)
        for n in range(block_rows):
            at = pl.ds(pl.multiple_of((block * block_rows + n) * pitch, 8), cols)
            sign[at] = v[n * cols : (n + 1) * cols]
        zsign[pl.ds(block * OUT_PITCH, 128)] = v.T
        return carry

    lax.fori_loop(0, blocks, signs, 0)

    there_count = sum(there.astype(jnp.int32) for there, _ in sides)
    pl.semaphore_wait(barrier, there_count)

    def one_stage(stage, field, fresh, finish):
        sends = []
        for direction, (src, src_at, dst, dst_at, count) in enumerate((
            (field, own, field, own + rows * pitch, own),
            (field, rows * pitch, field, 0, own),
            (yface, (stage * 2) * face, yhalo, (stage * 2 + 1) * face, face),
            (yface, (stage * 2 + 1) * face, yhalo, (stage * 2) * face, face),
        )):
            sends.append(pltpu.make_async_remote_copy(
                src_ref=src.at[pl.ds(src_at, count)],
                dst_ref=dst.at[pl.ds(dst_at, count)],
                send_sem=send_sem.at[stage * 4 + direction],
                recv_sem=recv_sem.at[stage * 4 + direction],
                device_id=sides[direction][1],
                device_id_type=MESH,
            ))
        for direction in (0, 1):
            @pl.when(sides[direction][0])
            def _(direction=direction):
                sends[direction].start()
        for side in range(2):
            for n in range(GHOST):
                y = n if side == 0 else cols - GHOST + n
                for x in range(0, rows, 8):
                    yface[pl.ds((stage * 2 + side) * face + n * rows + x, 8)] = field[
                        pl.ds(own + x * pitch + y, 8, stride=pitch)
                    ]
        for direction in (2, 3):
            @pl.when(sides[direction][0])
            def _(direction=direction):
                sends[direction].start()

        def flip(block, carry):
            v = [
                field[pl.ds(pl.multiple_of(own + (block * block_rows + n) * pitch, 8), cols)]
                for n in range(block_rows)
            ]
            zin[pl.ds(block * PITCH + ZPAD, 128)] = jnp.concatenate(v, axis=0).T
            return carry

        lax.fori_loop(0, blocks, flip, 0, unroll=True)

        def z_cell(group, z):
            return zin[pl.ds(group * 8 * PITCH + ZPAD + z, 8, stride=PITCH)]

        depth = 128

        def z_group(q, carry):
            state = begin([z_cell(q, z) for z in range(-3, 2)])
            first = push(state, z_cell(q, 2))

            def z_steps(index, carry):
                st, behind = carry
                for u in range(UNROLL):
                    z = index * UNROLL + u
                    st, next_behind, ahead = push(st, z_cell(q, z + 3))
                    at = pl.ds(q * 8 * OUT_PITCH + z, 8, stride=OUT_PITCH)
                    zout[at] = upwind(zsign[at], behind, ahead)
                    behind = next_behind
                return st, behind

            lax.fori_loop(0, depth // UNROLL, z_steps, first[:2])
            return carry

        lax.fori_loop(0, groups, z_group, 0)

        def unflip(block, carry):
            acc_z[pl.ds(pl.multiple_of(block * 128, 128), 128)] = zout[
                pl.ds(block * OUT_PITCH, 128)
            ].T
            return carry

        lax.fori_loop(0, blocks, unflip, 0, unroll=True)

        for direction, there in ((2, high_y), (3, low_y)):
            @pl.when(there)
            def _(direction=direction):
                sends[direction].wait_recv()

        def y_block(block, carry):
            x = block * 8

            def low_cell(n):
                return yhalo[pl.ds(pl.multiple_of((stage * 2) * face + n * rows + x, 8), 8)]

            def high_cell(n):
                return yhalo[pl.ds(pl.multiple_of((stage * 2 + 1) * face + n * rows + x, 8), 8)]

            def cell(y):
                return field[pl.ds(own + x * pitch + y, 8, stride=pitch)]

            def steps(start, count, carry, source):
                st, behind = carry
                for u in range(count):
                    st, next_behind, ahead = push(st, source(u))
                    at = pl.ds(x * pitch + start + u, 8, stride=pitch)
                    acc_y[at] = upwind(sign[at], behind, ahead)
                    behind = next_behind
                return st, behind

            st = begin([low_cell(n) for n in range(GHOST)] + [cell(0), cell(1)])
            carried = push(st, cell(2))[:2]
            trips = (cols - GHOST) // UNROLL
            carried = lax.fori_loop(
                0, trips,
                lambda i, c: steps(i * UNROLL, UNROLL, c, lambda u: cell(i * UNROLL + u + GHOST)),
                carried,
            )
            done = trips * UNROLL
            rest = cols - GHOST - done
            steps(done, rest + GHOST, carried, lambda u: (
                cell(done + u + GHOST) if u < rest else high_cell(u - rest)
            ))
            return carry

        lax.fori_loop(0, rows // 8, y_block, 0)

        for direction, there in ((0, high_x), (1, low_x)):
            @pl.when(there)
            def _(direction=direction):
                sends[direction].wait_recv()

        def x_block(block, carry):
            y = block * 8

            def cell(x):
                return field[spaced(x + GHOST, y)]

            st = begin([cell(x) for x in range(-3, 2)])
            carried = push(st, cell(2))[:2]

            def steps(index, carry):
                st, behind = carry
                for u in range(UNROLL):
                    x = index * UNROLL + u
                    st, next_behind, ahead = push(st, cell(x + 3))
                    at, here = spaced(x, y), natural(x, y)
                    total = upwind(sign[at], behind, ahead) + (acc_y[at] + acc_z[here])
                    moved = cell(x) - (speed[here] * STEP) * root(total)
                    fresh[spaced(x + GHOST, y)] = finish(moved, spaced(x + GHOST, y))
                    behind = next_behind
                return st, behind

            lax.fori_loop(0, rows // UNROLL, steps, carried)
            return carry

        lax.fori_loop(0, cols // 8, x_block, 0)

        for direction in range(4):
            @pl.when(sides[direction][0])
            def _(direction=direction):
                sends[direction].wait_send()

    def time_step(step, carry):
        last = jnp.where(step == RK_STEPS - 1, jnp.float32(0.5 / SCALE), jnp.float32(0.5))
        one_stage(2 * step, field_a, field_b, lambda moved, at: moved)
        one_stage(2 * step + 1, field_b, field_a, lambda moved, at: last * (field_a[at] + moved))
        return carry

    lax.fori_loop(0, RK_STEPS, time_step, 0)
    stores = []
    for x in range(rows):
        stores.append(pltpu.make_async_copy(
            field_a.at[pl.ds(own + x * pitch, cols)], out_ref.at[pl.ds(x * cols, cols)],
            store_sem.at[x],
        ))
        stores[-1].start()
    for store in stores:
        store.wait()


def advance(level_set, normal_speed, rows, cols, n_gx, n_gy):
    cells = rows * cols
    blocks = cells // 128
    pitch = cols + GAP
    flat = pltpu.VMEM((cells, 128), jnp.float32)
    spaced = pltpu.VMEM((rows * pitch, 128), jnp.float32)
    padded = pltpu.VMEM(((rows + 2 * GHOST) * pitch, 128), jnp.float32)
    return pl.pallas_call(
        functools.partial(advance_kernel, rows, cols, n_gx, n_gy),
        out_shape=jax.ShapeDtypeStruct((cells, 128), jnp.float32),
        in_specs=[pl.BlockSpec(memory_space=pltpu.HBM)] * 2,
        out_specs=pl.BlockSpec(memory_space=pl.ANY),
        scratch_shapes=[
            padded, padded, flat, spaced, spaced, flat,
            pltpu.VMEM((blocks * PITCH, 128), jnp.float32),
            pltpu.VMEM((blocks * OUT_PITCH, 128), jnp.float32),
            pltpu.VMEM((blocks * OUT_PITCH, 128), jnp.float32),
            pltpu.VMEM((STAGES * 2 * GHOST * rows, 128), jnp.float32),
            pltpu.VMEM((STAGES * 2 * GHOST * rows, 128), jnp.float32),
            pltpu.SemaphoreType.DMA((STAGES * 4,)),
            pltpu.SemaphoreType.DMA((STAGES * 4,)),
            pltpu.SemaphoreType.DMA((2 * PARTS,)),
            pltpu.SemaphoreType.DMA((rows,)),
        ],
        compiler_params=pltpu.CompilerParams(
            collective_id=0, has_side_effects=True, vmem_limit_bytes=28 * 2**20
        ),
        name="advance",
    )(level_set, normal_speed)


def reinit_kernel(rows, cols, field, band, out, t_a, t_b, gain, sign):
    wide = cols // TILE
    down = rows // TILE

    def source(i, j, d):
        return pl.ds((d * TILE + i) * cols + j, wide, stride=TILE)

    def gather(i, carry):
        for j in range(TILE):
            v = jnp.concatenate([field[source(i, j, d)] for d in range(down)], axis=0)
            at = pl.ds(pl.multiple_of((i * TILE + j) * 8, 8), 8)
            t_a[at] = v
            gain[at] = (0.3 * v) * lax.rsqrt(v * v + 1.0)
            sign[at] = jnp.where(v > 0.0, 1.0, -1.0)
        return carry

    lax.fori_loop(0, TILE, gather, 0)
    lane = lax.broadcasted_iota(jnp.int32, (8, 128), 1)
    first = lane == 0

    def sweep(now, later):
        def line(i, carry):
            above = jnp.maximum(i - 1, 0) * TILE
            below = jnp.minimum(i + 1, TILE - 1) * TILE
            here = i * TILE

            def cell(row, j):
                return now[pl.ds(pl.multiple_of((row + j) * 8, 8), 8)]

            values = [cell(here, j) for j in range(TILE)]
            for j in range(TILE):
                v = values[j]
                at = pl.ds(pl.multiple_of((here + j) * 8, 8), 8)
                s = sign[at]
                total = None
                mz = jnp.where(first, 0.0, v - pltpu.roll(v, 1, 1))
                pairs = [
                    (v - cell(above, j), v - cell(below, j)),
                    (v - values[max(j - 1, 0)], v - values[min(j + 1, TILE - 1)]),
                    (mz, -pltpu.roll(mz, 127, 1)),
                ]
                for m, nq in pairs:
                    u = jnp.maximum(jnp.maximum(s * m, s * nq), 0.0)
                    total = u * u if total is None else total + u * u
                later[at] = v - gain[at] * (root(total) - 1.0)
            return carry

        lax.fori_loop(0, TILE, line, 0)

    def sweeps(index, carry):
        sweep(t_a, t_b)
        sweep(t_b, t_a)
        return carry

    lax.fori_loop(0, REINIT // 2, sweeps, 0)

    def scatter(i, carry):
        for j in range(TILE):
            v = t_a[pl.ds(pl.multiple_of((i * TILE + j) * 8, 8), 8)]
            for d in range(down):
                at = source(i, j, d)
                mask = band[pl.ds(d * wide, wide)]
                out[at] = jnp.where(mask > 0, v[d * wide : (d + 1) * wide], field[at])
        return carry

    lax.fori_loop(0, TILE, scatter, 0)


def reinitialize(field, band, rows, cols):
    cells = rows * cols
    flat = pltpu.VMEM((cells, 128), jnp.float32)
    return pl.pallas_call(
        functools.partial(reinit_kernel, rows, cols),
        out_shape=jax.ShapeDtypeStruct((cells, 128), jnp.float32),
        in_specs=[pl.BlockSpec(memory_space=pltpu.VMEM)] * 2,
        out_specs=pl.BlockSpec(memory_space=pltpu.VMEM),
        scratch_shapes=[flat, flat, flat, flat],
        compiler_params=pltpu.CompilerParams(vmem_limit_bytes=24 * 2**20),
        name="reinitialize",
    )(field, band)


def solution(mesh):
    n_gx, n_gy = mesh.shape["gx"], mesh.shape["gy"]

    def body(level_set, normal_speed, band_tiles):
        rows, cols, depth = level_set.shape
        cells = rows * cols
        field = advance(
            level_set.reshape(cells, depth), normal_speed.reshape(cells, depth),
            rows, cols, n_gx, n_gy,
        )
        band = jnp.broadcast_to(band_tiles.reshape(-1, 1), (band_tiles.size, 128))
        return reinitialize(field, band, rows, cols).reshape(rows, cols, depth)

    return jax.shard_map(
        body,
        mesh=mesh,
        in_specs=(
            P(("groups", "gx"), "gy", None),
            P(("groups", "gx"), "gy", None),
            P(("groups", "gx"), "gy"),
        ),
        out_specs=P(("groups", "gx"), "gy", None),
        check_vma=False,
    )
```

```python
import functools

import jax
import jax.numpy as jnp
from jax import lax
from jax.experimental import pallas as pl
from jax.experimental.pallas import tpu as pltpu
from jax.sharding import PartitionSpec as P

TILE = 16
RK_STEPS = 2
REINIT = 12
STAGES = 2 * RK_STEPS
GHOST = 3
SCALE = 1.5 ** 0.5
STEP = 0.125
EPS = 0.375e-6
TINY = 1e-37
FLOOR = 1e-18
PITCH = 140
OUT_PITCH = 132
ZPAD = 4
GAP = 8
Z_STEPS = 32
Y_TRIPS = 2
PARTS = 4
MESH = pl.DeviceIdType.MESH


def rcp(x):
    return pl.reciprocal(x, approx=True)


def root(x):
    return x * lax.rsqrt(jnp.maximum(x, TINY))


def stencil(e, f, half_x, half_y):
    mid = e * f + (half_x * half_y + EPS)
    rl = rcp(mid + half_y * e)
    rr = rcp(mid - half_x * e)
    rm = rcp(mid)
    return rl * rl, (rm * rm) * 6.0, rr * rr


def push(state, phi):
    last_phi, last_d, last_pair, older_pair, last_g, last_half, last_f, delta, a, left, b = state
    d = phi - last_phi
    g = d - last_d
    pair = d + last_d
    half = g * 0.5
    e = g - last_g
    f = e * (1.0 / 3.0)
    next_delta = last_f - f
    next_left, next_mid, w = stencil(e, f, last_half, half)
    aa = a * delta
    ww = w * next_delta
    both = aa + ww
    both = both + both
    weights = a + b + w
    behind = (last_pair - last_f) + (both + ww) * rcp(weights + (w + w))
    ahead = (both + aa) * rcp(weights + (a + a)) - (older_pair - last_f)
    state = (phi, d, pair, last_pair, g, half, f, next_delta, left, next_left, next_mid)
    return state, behind, ahead


def begin(cells):
    p0, p1, p2, p3, p4 = cells
    d1, d2, d3, d4 = p1 - p0, p2 - p1, p3 - p2, p4 - p3
    g1, g2, g3 = d2 - d1, d3 - d2, d4 - d3
    h1, h2, h3 = g1 * 0.5, g2 * 0.5, g3 * 0.5
    e1, e2 = g2 - g1, g3 - g2
    f1, f2 = e1 * (1.0 / 3.0), e2 * (1.0 / 3.0)
    left_a, _, _ = stencil(e1, f1, h1, h2)
    left_b, mid_b, _ = stencil(e2, f2, h2, h3)
    return (p4, d4, d4 + d3, d3 + d2, g3, h3, f2, f1 - f2, left_a, left_b, mid_b)


def upwind(sign, behind, ahead):
    v = jnp.maximum(jnp.maximum(sign * behind, sign * ahead), 0.0)
    return v * v


def advance_kernel(
    rows, cols, n_gx, n_gy,
    level_hbm, speed_hbm, out_ref,
    field_a, field_b, kept, speed, rate, sign, acc_y, acc_z, zin, zout, zsign, yface, yhalo,
    send_sem, recv_sem, local_sem,
):
    cells = rows * cols
    pitch = cols + GAP
    own = GHOST * pitch
    blocks = cells // 128
    block_rows = 128 // cols
    groups = blocks // 8
    face = GHOST * rows
    gx = lax.axis_index("gx")
    gy = lax.axis_index("gy")
    low_x, high_x = gx > 0, gx < n_gx - 1
    low_y, high_y = gy > 0, gy < n_gy - 1
    sides = (
        (low_x, {"gx": gx - 1}), (high_x, {"gx": gx + 1}),
        (low_y, {"gy": gy - 1}), (high_y, {"gy": gy + 1}),
    )

    part = cells // PARTS
    loads = []
    for n in range(PARTS):
        at = pl.ds(n * part, part)
        loads.append((
            pltpu.make_async_copy(level_hbm.at[at], acc_z.at[at], local_sem.at[n]),
            pltpu.make_async_copy(speed_hbm.at[at], speed.at[at], local_sem.at[PARTS + n]),
        ))
    for level, _ in loads:
        level.start()
    for _, moving in loads:
        moving.start()

    barrier = pltpu.get_barrier_semaphore()
    for there, device in sides:
        @pl.when(there)
        def _():
            pl.semaphore_signal(barrier, inc=1, device_id=device, device_id_type=MESH)

    zero = jnp.zeros((own, 128), jnp.float32)
    gap = jnp.zeros((GAP, 128), jnp.float32)
    for field in (field_a, field_b):
        for x in range(rows):
            field[pl.ds(own + x * pitch + cols, GAP)] = gap

        @pl.when(jnp.logical_not(low_x))
        def _():
            field[pl.ds(0, own)] = zero

        @pl.when(jnp.logical_not(high_x))
        def _():
            field[pl.ds(own + rows * pitch, own)] = zero

    for stage in range(STAGES):
        @pl.when(jnp.logical_not(low_y))
        def _():
            yhalo[pl.ds((stage * 2) * face, face)] = zero[:face]

        @pl.when(jnp.logical_not(high_y))
        def _():
            yhalo[pl.ds((stage * 2 + 1) * face, face)] = zero[:face]

    for q in range(groups):
        for block in range(8):
            at = block * PITCH
            zin[q][pl.ds(at, ZPAD)] = gap[:ZPAD]
            zin[q][pl.ds(at + ZPAD + 128, PITCH - 128 - ZPAD)] = gap[: PITCH - 128 - ZPAD]

    def natural(x, y):
        return pl.ds(pl.multiple_of(x * cols + y, 8), 8)

    def spaced(x, y):
        return pl.ds(pl.multiple_of(x * pitch + y, 8), 8)

    for level, _ in loads:
        level.wait()

    def scaled(x, carry):
        field_a[pl.ds(pl.multiple_of(own + x * pitch, 8), cols)] = (
            acc_z[pl.ds(pl.multiple_of(x * cols, 8), cols)] * SCALE
        )
        return carry

    lax.fori_loop(0, rows, scaled, 0, unroll=True)
    for _, moving in loads:
        moving.wait()

    def signs(block, carry):
        here = pl.ds(pl.multiple_of(block * 128, 128), 128)
        v = jnp.where(speed[here] > 0.0, 1.0, -1.0)
        rate[here] = speed[here] * STEP
        for n in range(block_rows):
            at = pl.ds(pl.multiple_of((block * block_rows + n) * pitch, 8), cols)
            sign[at] = v[n * cols : (n + 1) * cols]
        return v

    for q in range(groups):
        def sign_block(block, carry):
            v = signs(q * 8 + block, carry)
            zsign[q][pl.ds(block * OUT_PITCH, 128)] = v.T
            return carry

        lax.fori_loop(0, 8, sign_block, 0, unroll=True)

    there_count = sum(there.astype(jnp.int32) for there, _ in sides)
    pl.semaphore_wait(barrier, there_count)

    def one_stage(stage, field, write):
        sends = []
        for direction, (src, src_at, dst, dst_at, count) in enumerate((
            (field, own, field, own + rows * pitch, own),
            (field, rows * pitch, field, 0, own),
            (yface, (stage * 2) * face, yhalo, (stage * 2 + 1) * face, face),
            (yface, (stage * 2 + 1) * face, yhalo, (stage * 2) * face, face),
        )):
            sends.append(pltpu.make_async_remote_copy(
                src_ref=src.at[pl.ds(src_at, count)],
                dst_ref=dst.at[pl.ds(dst_at, count)],
                send_sem=send_sem.at[stage * 4 + direction],
                recv_sem=recv_sem.at[stage * 4 + direction],
                device_id=sides[direction][1],
                device_id_type=MESH,
            ))
        for direction in (0, 1):
            @pl.when(sides[direction][0])
            def _(direction=direction):
                sends[direction].start()
        for side in range(2):
            for n in range(GHOST):
                y = n if side == 0 else cols - GHOST + n
                for x in range(0, rows, 8):
                    yface[pl.ds((stage * 2 + side) * face + n * rows + x, 8)] = field[
                        pl.ds(own + x * pitch + y, 8, stride=pitch)
                    ]
        for direction in (2, 3):
            @pl.when(sides[direction][0])
            def _(direction=direction):
                sends[direction].start()

        def flip(q, block):
            v = []
            for n in range(block_rows):
                x = (q * 8 + block) * block_rows + n
                v.append(field[pl.ds(pl.multiple_of(own + x * pitch, 8), cols)])
            zin[q][pl.ds(block * PITCH + ZPAD, 128)] = jnp.concatenate(v, axis=0).T

        def unflip(q, block):
            acc_z[pl.ds(pl.multiple_of((q * 8 + block) * 128, 128), 128)] = zout[q][
                pl.ds(block * OUT_PITCH, 128)
            ].T

        def flip_first(block, carry):
            flip(0, block)
            return carry

        lax.fori_loop(0, 8, flip_first, 0, unroll=True)
        trips = 128 // Z_STEPS
        for q in range(groups):
            def z_cell(z):
                return zin[q][pl.ds(ZPAD + z, 8, stride=PITCH)]

            def z_trip(trip, carry):
                def step(u, carry):
                    st, behind = carry
                    z = trip * Z_STEPS + u
                    st, next_behind, ahead = push(st, z_cell(z + 3))
                    at = pl.ds(z, 8, stride=OUT_PITCH)
                    zout[q][at] = upwind(zsign[q][at], behind, ahead)
                    return st, next_behind

                for n in range(8 // trips):
                    if q + 1 < groups:
                        flip(q + 1, trip * (8 // trips) + n)
                    if q > 0:
                        unflip(q - 1, trip * (8 // trips) + n)
                return lax.fori_loop(0, Z_STEPS, step, carry, unroll=True)

            first = push(begin([z_cell(z) for z in range(-3, 2)]), z_cell(2))
            lax.fori_loop(0, trips, z_trip, first[:2])

        for direction, there in ((2, high_y), (3, low_y)):
            @pl.when(there)
            def _(direction=direction):
                sends[direction].wait_recv()

        def y_block(block, carry):
            x = block * 8

            def low_cell(n):
                return yhalo[pl.ds(pl.multiple_of((stage * 2) * face + n * rows + x, 8), 8)]

            def high_cell(n):
                return yhalo[pl.ds(pl.multiple_of((stage * 2 + 1) * face + n * rows + x, 8), 8)]

            def cell(y):
                return field[pl.ds(own + x * pitch + y, 8, stride=pitch)]

            def step(y, carry, phi):
                st, behind = carry
                st, next_behind, ahead = push(st, phi)
                at = pl.ds(x * pitch + y, 8, stride=pitch)
                acc_y[at] = upwind(sign[at], behind, ahead)
                return st, next_behind

            st = begin([low_cell(n) for n in range(GHOST)] + [cell(0), cell(1)])
            carried = push(st, cell(2))[:2]
            count = (cols - GHOST) // Y_TRIPS

            def y_trip(trip, carried):
                unflip(groups - 1, block * Y_TRIPS + trip)
                start = trip * count
                return lax.fori_loop(
                    0, count,
                    lambda u, c: step(start + u, c, cell(start + u + GHOST)),
                    carried, unroll=True,
                )

            carried = lax.fori_loop(0, Y_TRIPS, y_trip, carried)
            for y in range(count * Y_TRIPS, cols):
                ahead = y + GHOST
                phi = cell(ahead) if ahead < cols else high_cell(ahead - cols)
                carried = step(y, carried, phi)
            return carry

        lax.fori_loop(0, rows // 8, y_block, 0)

        for direction, there in ((0, high_x), (1, low_x)):
            @pl.when(there)
            def _(direction=direction):
                sends[direction].wait_recv()

        def x_block(block, carry):
            y = block * 8

            def cell(x):
                return field[spaced(x + GHOST, y)]

            st = begin([cell(x) for x in range(-3, 2)])
            carried = push(st, cell(2))[:2]

            def step(x, carry):
                st, behind = carry
                st, next_behind, ahead = push(st, cell(x + 3))
                at, here = spaced(x, y), natural(x, y)
                total = upwind(sign[at], behind, ahead) + (acc_y[at] + acc_z[here])
                now = cell(x)
                write(now, now - rate[here] * root(total), spaced(x + GHOST, y), here)
                return st, next_behind

            lax.fori_loop(0, rows, step, carried, unroll=True)
            return carry

        lax.fori_loop(0, cols // 8, x_block, 0)

        for direction in range(4):
            @pl.when(sides[direction][0])
            def _(direction=direction):
                sends[direction].wait_send()

    def time_step(step, carry):
        last = jnp.where(step == RK_STEPS - 1, jnp.float32(0.5 / SCALE), jnp.float32(0.5))

        def halfway(now, moved, at, here):
            field_b[at] = moved
            kept[here] = now

        def whole(now, moved, at, here):
            result = last * (kept[here] + moved)
            field_a[at] = result
            out_ref[here] = result

        one_stage(2 * step, field_a, halfway)
        one_stage(2 * step + 1, field_b, whole)
        return carry

    lax.fori_loop(0, RK_STEPS, time_step, 0)


def advance(level_set, normal_speed, rows, cols, n_gx, n_gy):
    cells = rows * cols
    groups = cells // 1024
    pitch = cols + GAP
    flat = pltpu.VMEM((cells, 128), jnp.float32)
    spaced = pltpu.VMEM((rows * pitch, 128), jnp.float32)
    padded = pltpu.VMEM(((rows + 2 * GHOST) * pitch, 128), jnp.float32)
    return pl.pallas_call(
        functools.partial(advance_kernel, rows, cols, n_gx, n_gy),
        out_shape=jax.ShapeDtypeStruct((cells, 128), jnp.float32),
        in_specs=[pl.BlockSpec(memory_space=pltpu.HBM)] * 2,
        out_specs=pl.BlockSpec(memory_space=pltpu.VMEM),
        scratch_shapes=[
            padded, padded, flat, flat, flat, spaced, spaced, flat,
            [pltpu.VMEM((8 * PITCH, 128), jnp.float32)] * groups,
            [pltpu.VMEM((8 * OUT_PITCH, 128), jnp.float32)] * groups,
            [pltpu.VMEM((8 * OUT_PITCH, 128), jnp.float32)] * groups,
            pltpu.VMEM((STAGES * 2 * GHOST * rows, 128), jnp.float32),
            pltpu.VMEM((STAGES * 2 * GHOST * rows, 128), jnp.float32),
            pltpu.SemaphoreType.DMA((STAGES * 4,)),
            pltpu.SemaphoreType.DMA((STAGES * 4,)),
            pltpu.SemaphoreType.DMA((2 * PARTS,)),
        ],
        compiler_params=pltpu.CompilerParams(
            collective_id=0, has_side_effects=True, vmem_limit_bytes=28 * 2**20
        ),
        name="advance",
    )(level_set, normal_speed)


def reinit_kernel(rows, cols, field, band, out, t_a, t_b, gain, sign, store_sem, merged):
    wide = cols // TILE
    down = rows // TILE
    lane = lax.broadcasted_iota(jnp.int32, (8, 128), 1)
    inner = jnp.where(lane == 0, 0.0, 1.0)
    slot = lax.broadcasted_iota(jnp.int32, (8, 128), 0)
    chosen = jnp.zeros((8, 128), jnp.int32)
    for d in range(down):
        for w in range(wide):
            chosen = jnp.where(slot == d * wide + w, band[d, w], chosen)

    def source(i, j, d):
        return pl.ds((d * TILE + i) * cols + j, wide, stride=TILE)

    def place(i, j):
        return pl.ds(pl.multiple_of((i * TILE + j) * 8, 8), 8)

    def gather(i, carry):
        for j in range(TILE):
            v = jnp.concatenate([field[source(i, j, d)] for d in range(down)], axis=0)
            t_a[place(i, j)] = v
            gain[place(i, j)] = (0.3 * v) * lax.rsqrt(v * v + 1.0)
            sign[place(i, j)] = jnp.where(v > 0.0, 1.0, -1.0)
        return carry

    lax.fori_loop(0, TILE, gather, 0)

    def sweep(now, later):
        zero = jnp.zeros((8, 128), jnp.float32)
        above = [zero] * TILE
        values = [now[place(0, j)] for j in range(TILE)]
        for i in range(TILE):
            next_values = [now[place(i + 1, j)] for j in range(TILE)] if i + 1 < TILE else values
            left = zero
            next_above = []
            for j in range(TILE):
                v = values[j]
                s = sign[place(i, j)]
                below = next_values[j] - v
                right = values[j + 1] - v if j + 1 < TILE else zero
                back = (v - pltpu.roll(v, 1, 1)) * inner
                total = None
                for m, q in ((above[j], below), (left, right), (back, pltpu.roll(back, 127, 1))):
                    floor = FLOOR if total is None else 0.0
                    u = jnp.maximum(jnp.maximum(s * m, -s * q), floor)
                    total = u * u if total is None else total + u * u
                later[place(i, j)] = v - gain[place(i, j)] * (total * lax.rsqrt(total) - 1.0)
                next_above.append(below)
                left = right
            above, values = next_above, next_values

    def sweeps(index, carry):
        sweep(t_a, t_b)
        sweep(t_b, t_a)
        return carry

    lax.fori_loop(0, REINIT // 2, sweeps, 0)

    def copy_out(i, d):
        at = pl.ds(pl.multiple_of((d * TILE + i) * cols, 8), cols)
        return pltpu.make_async_copy(merged.at[at], out.at[at], store_sem.at[d * TILE + i])

    def scatter(i, carry):
        for j in range(TILE):
            v = t_a[place(i, j)]
            for d in range(down):
                at = source(i, j, d)
                part = slice(d * wide, (d + 1) * wide)
                merged[at] = jnp.where(chosen[part] > 0, v[part], field[at])
        for d in range(down):
            copy_out(i, d).start()
        return carry

    lax.fori_loop(0, TILE, scatter, 0)

    def finish(i, carry):
        for d in range(down):
            copy_out(i, d).wait()
        return carry

    lax.fori_loop(0, TILE, finish, 0)


def reinitialize(field, band, rows, cols):
    cells = rows * cols
    flat = pltpu.VMEM((cells, 128), jnp.float32)
    return pl.pallas_call(
        functools.partial(reinit_kernel, rows, cols),
        out_shape=jax.ShapeDtypeStruct((cells, 128), jnp.float32),
        in_specs=[
            pl.BlockSpec(memory_space=pltpu.VMEM),
            pl.BlockSpec(memory_space=pltpu.SMEM),
        ],
        out_specs=pl.BlockSpec(memory_space=pltpu.HBM),
        scratch_shapes=[flat, flat, flat, flat, pltpu.SemaphoreType.DMA((rows,)), flat],
        compiler_params=pltpu.CompilerParams(vmem_limit_bytes=24 * 2**20),
        name="reinitialize",
    )(field, band)


def solution(mesh):
    n_gx, n_gy = mesh.shape["gx"], mesh.shape["gy"]

    def body(level_set, normal_speed, band_tiles):
        rows, cols, depth = level_set.shape
        cells = rows * cols
        field = advance(
            level_set.reshape(cells, depth), normal_speed.reshape(cells, depth),
            rows, cols, n_gx, n_gy,
        )
        return reinitialize(field, band_tiles, rows, cols).reshape(rows, cols, depth)

    return jax.shard_map(
        body,
        mesh=mesh,
        in_specs=(
            P(("groups", "gx"), "gy", None),
            P(("groups", "gx"), "gy", None),
            P(("groups", "gx"), "gy"),
        ),
        out_specs=P(("groups", "gx"), "gy", None),
        check_vma=False,
    )
```

```python
import functools

import jax
import jax.numpy as jnp
from jax import lax
from jax.experimental import pallas as pl
from jax.experimental.pallas import tpu as pltpu
from jax.sharding import PartitionSpec as P

TILE = 16
RK_STEPS = 2
REINIT = 12
STAGES = 2 * RK_STEPS
GHOST = 3
SCALE = 1.5 ** 0.5
STEP = 0.125
EPS = 0.375e-6
TINY = 1e-37
FLOOR = 1e-18
PITCH = 140
OUT_PITCH = 132
ZPAD = 4
GAP = 8
Z_STEPS = 64
CHUNKS = 4
MESH = pl.DeviceIdType.MESH


def rcp(x):
    return pl.reciprocal(x, approx=True)


def root(x):
    return x * lax.rsqrt(jnp.maximum(x, TINY))


def stencil(e, f, half_x, half_y):
    mid = e * f + (half_x * half_y + EPS)
    rl = rcp(mid + half_y * e)
    rr = rcp(mid - half_x * e)
    rm = rcp(mid)
    return rl * rl, (rm * rm) * 6.0, rr * rr


def push(state, phi):
    last_phi, last_d, last_pair, older_pair, last_g, last_half, last_f, delta, a, left, b = state
    d = phi - last_phi
    g = d - last_d
    pair = d + last_d
    half = g * 0.5
    e = g - last_g
    f = e * (1.0 / 3.0)
    next_delta = last_f - f
    next_left, next_mid, w = stencil(e, f, last_half, half)
    aa = a * delta
    ww = w * next_delta
    both = aa + ww
    both = both + both
    weights = a + b + w
    behind = (last_pair - last_f) + (both + ww) * rcp(weights + (w + w))
    ahead = (both + aa) * rcp(weights + (a + a)) - (older_pair - last_f)
    state = (phi, d, pair, last_pair, g, half, f, next_delta, left, next_left, next_mid)
    return state, behind, ahead


def begin(cells):
    p0, p1, p2, p3, p4 = cells
    d1, d2, d3, d4 = p1 - p0, p2 - p1, p3 - p2, p4 - p3
    g1, g2, g3 = d2 - d1, d3 - d2, d4 - d3
    h1, h2, h3 = g1 * 0.5, g2 * 0.5, g3 * 0.5
    e1, e2 = g2 - g1, g3 - g2
    f1, f2 = e1 * (1.0 / 3.0), e2 * (1.0 / 3.0)
    left_a, _, _ = stencil(e1, f1, h1, h2)
    left_b, mid_b, _ = stencil(e2, f2, h2, h3)
    return (p4, d4, d4 + d3, d3 + d2, g3, h3, f2, f1 - f2, left_a, left_b, mid_b)


def upwind(sign, behind, ahead):
    v = jnp.maximum(jnp.maximum(sign * behind, sign * ahead), 0.0)
    return v * v


def advance_kernel(
    rows, cols, n_gx, n_gy,
    level, speed, out_ref,
    field_a, field_b, kept, rate, sign, acc_y, acc_z, zin, zout, zsign,
    xface, xhalo, yface, yhalo, x_send, x_recv, y_send, y_recv,
):
    cells = rows * cols
    pitch = cols + GAP
    blocks = cells // 128
    block_rows = 128 // cols
    groups = blocks // 8
    face = GHOST * rows
    slab = cols // CHUNKS
    xface_rows = GHOST * slab
    gx = lax.axis_index("gx")
    gy = lax.axis_index("gy")
    low_x, high_x = gx > 0, gx < n_gx - 1
    low_y, high_y = gy > 0, gy < n_gy - 1
    sides = (
        (low_x, {"gx": gx - 1}), (high_x, {"gx": gx + 1}),
        (low_y, {"gy": gy - 1}), (high_y, {"gy": gy + 1}),
    )

    barrier = pltpu.get_barrier_semaphore()
    for there, device in sides:
        @pl.when(there)
        def _():
            pl.semaphore_signal(barrier, inc=1, device_id=device, device_id_type=MESH)

    gap = jnp.zeros((GAP, 128), jnp.float32)
    x_zero = jnp.zeros((CHUNKS * xface_rows, 128), jnp.float32)
    y_zero = jnp.zeros((face, 128), jnp.float32)
    for stage in range(STAGES):
        for side, (there, _) in enumerate(sides[:2]):
            @pl.when(jnp.logical_not(there))
            def _(at=(stage * 2 + side) * CHUNKS * xface_rows):
                xhalo[pl.ds(at, CHUNKS * xface_rows)] = x_zero

        for side, (there, _) in enumerate(sides[2:]):
            @pl.when(jnp.logical_not(there))
            def _(at=(stage * 2 + side) * face):
                yhalo[pl.ds(at, face)] = y_zero

    for q in range(groups):
        for block in range(8):
            at = block * PITCH
            zin[q][pl.ds(at, ZPAD)] = gap[:ZPAD]
            zin[q][pl.ds(at + ZPAD + 128, PITCH - 128 - ZPAD)] = gap[: PITCH - 128 - ZPAD]

    def natural(x, y):
        return pl.ds(pl.multiple_of(x * cols + y, 8), 8)

    def spaced(x, y):
        return pl.ds(pl.multiple_of(x * pitch + y, 8), 8)

    def x_at(stage, side, chunk):
        return ((stage * 2 + side) * CHUNKS + chunk) * xface_rows

    def x_copy(stage, side, chunk):
        sem = (stage * 2 + side) * CHUNKS + chunk
        return pltpu.make_async_remote_copy(
            src_ref=xface.at[pl.ds(pl.multiple_of(x_at(stage, side, chunk), 8), xface_rows)],
            dst_ref=xhalo.at[pl.ds(pl.multiple_of(x_at(stage, 1 - side, chunk), 8), xface_rows)],
            send_sem=x_send.at[sem],
            recv_sem=x_recv.at[sem],
            device_id=sides[side][1],
            device_id_type=MESH,
        )

    def y_copy(stage, side):
        return pltpu.make_async_remote_copy(
            src_ref=yface.at[pl.ds((stage * 2 + side) * face, face)],
            dst_ref=yhalo.at[pl.ds((stage * 2 + 1 - side) * face, face)],
            send_sem=y_send.at[stage * 2 + side],
            recv_sem=y_recv.at[stage * 2 + side],
            device_id=sides[2 + side][1],
            device_id_type=MESH,
        )

    def x_start(field, stage, chunk):
        for side in range(2):
            for n in range(GHOST):
                x = n if side == 0 else rows - GHOST + n
                for y in range(0, slab, 8):
                    at = pl.multiple_of(x_at(stage, side, chunk) + n * slab + y, 8)
                    xface[pl.ds(at, 8)] = field[spaced(x, chunk * slab + y)]
        for side in range(2):
            @pl.when(sides[side][0])
            def _(side=side):
                x_copy(stage, side, chunk).start()

    def scaled(x, carry):
        field_a[pl.ds(pl.multiple_of(x * pitch, 8), cols)] = (
            level[pl.ds(pl.multiple_of(x * cols, 8), cols)] * SCALE
        )
        return carry

    lax.fori_loop(0, rows, scaled, 0, unroll=True)

    there_count = sum(there.astype(jnp.int32) for there, _ in sides)
    pl.semaphore_wait(barrier, there_count)

    def first_chunk(chunk, carry):
        x_start(field_a, 0, chunk)
        return carry

    lax.fori_loop(0, CHUNKS, first_chunk, 0)

    def signs(block, carry):
        here = pl.ds(pl.multiple_of(block * 128, 128), 128)
        v = jnp.where(speed[here] > 0.0, 1.0, -1.0)
        rate[here] = speed[here] * STEP
        for n in range(block_rows):
            at = pl.ds(pl.multiple_of((block * block_rows + n) * pitch, 8), cols)
            sign[at] = v[n * cols : (n + 1) * cols]
        return v

    for q in range(groups):
        def sign_block(block, carry):
            v = signs(q * 8 + block, carry)
            zsign[q][pl.ds(block * OUT_PITCH, 128)] = v.T
            return carry

        lax.fori_loop(0, 8, sign_block, 0, unroll=True)

    def one_stage(stage, field, fresh, write, more):
        for side in range(2):
            for n in range(GHOST):
                y = n if side == 0 else cols - GHOST + n
                for x in range(0, rows, 8):
                    yface[pl.ds((stage * 2 + side) * face + n * rows + x, 8)] = field[
                        pl.ds(x * pitch + y, 8, stride=pitch)
                    ]
        for side in range(2):
            @pl.when(sides[2 + side][0])
            def _(side=side):
                y_copy(stage, side).start()

        def flip(q, block):
            v = []
            for n in range(block_rows):
                x = (q * 8 + block) * block_rows + n
                v.append(field[pl.ds(pl.multiple_of(x * pitch, 8), cols)])
            zin[q][pl.ds(block * PITCH + ZPAD, 128)] = jnp.concatenate(v, axis=0).T

        def unflip(q, block):
            acc_z[pl.ds(pl.multiple_of((q * 8 + block) * 128, 128), 128)] = zout[q][
                pl.ds(block * OUT_PITCH, 128)
            ].T

        def flip_first(block, carry):
            flip(0, block)
            return carry

        lax.fori_loop(0, 8, flip_first, 0, unroll=True)
        trips = 128 // Z_STEPS
        for q in range(groups):
            def z_cell(z):
                return zin[q][pl.ds(ZPAD + z, 8, stride=PITCH)]

            def z_trip(trip, carry):
                def step(u, carry):
                    st, behind = carry
                    z = trip * Z_STEPS + u
                    st, next_behind, ahead = push(st, z_cell(z + 3))
                    at = pl.ds(z, 8, stride=OUT_PITCH)
                    zout[q][at] = upwind(zsign[q][at], behind, ahead)
                    return st, next_behind

                for n in range(8 // trips):
                    if q + 1 < groups:
                        flip(q + 1, trip * (8 // trips) + n)
                    if q > 0:
                        unflip(q - 1, trip * (8 // trips) + n)
                return lax.fori_loop(0, Z_STEPS, step, carry, unroll=True)

            first = push(begin([z_cell(z) for z in range(-3, 2)]), z_cell(2))
            lax.fori_loop(0, trips, z_trip, first[:2])

        for side in range(2):
            @pl.when(sides[2 + side][0])
            def _(side=side):
                y_copy(stage, 1 - side).wait_recv()

        def y_block(block, carry):
            x = block * 8

            def low_cell(n):
                return yhalo[pl.ds(pl.multiple_of((stage * 2) * face + n * rows + x, 8), 8)]

            def high_cell(n):
                return yhalo[pl.ds(pl.multiple_of((stage * 2 + 1) * face + n * rows + x, 8), 8)]

            def cell(y):
                return field[pl.ds(x * pitch + y, 8, stride=pitch)]

            def step(y, carry, phi):
                st, behind = carry
                st, next_behind, ahead = push(st, phi)
                at = pl.ds(x * pitch + y, 8, stride=pitch)
                acc_y[at] = upwind(sign[at], behind, ahead)
                return st, next_behind

            st = begin([low_cell(n) for n in range(GHOST)] + [cell(0), cell(1)])
            carried = push(st, cell(2))[:2]
            for n in range(8 // (rows // 8)):
                unflip(groups - 1, block * (8 // (rows // 8)) + n)
            carried = lax.fori_loop(
                0, cols - GHOST, lambda y, c: step(y, c, cell(y + GHOST)), carried, unroll=True
            )
            for n in range(GHOST):
                carried = step(cols - GHOST + n, carried, high_cell(n))
            return carry

        lax.fori_loop(0, rows // 8, y_block, 0)

        def x_block(chunk, y):
            def cell(x):
                return field[spaced(x, chunk * slab + y)]

            def ghost(side, n):
                at = x_at(stage, side, chunk) + n * slab + y
                return xhalo[pl.ds(pl.multiple_of(at, 8), 8)]

            def step(x, carry, phi):
                st, behind = carry
                st, next_behind, ahead = push(st, phi)
                at, here = spaced(x, chunk * slab + y), natural(x, chunk * slab + y)
                total = upwind(sign[at], behind, ahead) + (acc_y[at] + acc_z[here])
                now = cell(x)
                write(now, now - rate[here] * root(total), at, here)
                return st, next_behind

            st = begin([ghost(0, n) for n in range(GHOST)] + [cell(0), cell(1)])
            carried = push(st, cell(2))[:2]
            carried = lax.fori_loop(
                0, rows - GHOST, lambda x, c: step(x, c, cell(x + GHOST)), carried, unroll=True
            )
            for n in range(GHOST):
                carried = step(rows - GHOST + n, carried, ghost(1, n))

        def x_chunk(chunk, carry):
            for side in range(2):
                @pl.when(sides[side][0])
                def _(side=side):
                    x_copy(stage, 1 - side, chunk).wait_recv()
            for y in range(0, slab, 8):
                x_block(chunk, y)

            @pl.when(more)
            def _():
                x_start(fresh, stage + 1, chunk)
            return carry

        lax.fori_loop(0, CHUNKS, x_chunk, 0)

    def time_step(step, carry):
        last = jnp.where(step == RK_STEPS - 1, jnp.float32(0.5 / SCALE), jnp.float32(0.5))

        def halfway(now, moved, at, here):
            field_b[at] = moved
            kept[here] = now

        def whole(now, moved, at, here):
            result = last * (kept[here] + moved)
            field_a[at] = result
            out_ref[here] = result

        one_stage(2 * step, field_a, field_b, halfway, True)
        one_stage(2 * step + 1, field_b, field_a, whole, step < RK_STEPS - 1)
        return carry

    lax.fori_loop(0, RK_STEPS, time_step, 0)

    def sent(stage, carry):
        for side in range(2):
            @pl.when(sides[side][0])
            def _(side=side):
                for chunk in range(CHUNKS):
                    x_copy(stage, side, chunk).wait_send()

            @pl.when(sides[2 + side][0])
            def _(side=side):
                y_copy(stage, side).wait_send()
        return carry

    lax.fori_loop(0, STAGES, sent, 0)


def advance(level_set, normal_speed, rows, cols, n_gx, n_gy):
    cells = rows * cols
    groups = cells // 1024
    pitch = cols + GAP
    flat = pltpu.VMEM((cells, 128), jnp.float32)
    spaced = pltpu.VMEM((rows * pitch, 128), jnp.float32)
    return pl.pallas_call(
        functools.partial(advance_kernel, rows, cols, n_gx, n_gy),
        out_shape=jax.ShapeDtypeStruct((cells, 128), jnp.float32),
        in_specs=[pl.BlockSpec(memory_space=pltpu.VMEM)] * 2,
        out_specs=pl.BlockSpec(memory_space=pltpu.VMEM),
        scratch_shapes=[
            spaced, spaced, flat, flat, spaced, spaced, flat,
            [pltpu.VMEM((8 * PITCH, 128), jnp.float32)] * groups,
            [pltpu.VMEM((8 * OUT_PITCH, 128), jnp.float32)] * groups,
            [pltpu.VMEM((8 * OUT_PITCH, 128), jnp.float32)] * groups,
            pltpu.VMEM((STAGES * 2 * GHOST * cols, 128), jnp.float32),
            pltpu.VMEM((STAGES * 2 * GHOST * cols, 128), jnp.float32),
            pltpu.VMEM((STAGES * 2 * GHOST * rows, 128), jnp.float32),
            pltpu.VMEM((STAGES * 2 * GHOST * rows, 128), jnp.float32),
            pltpu.SemaphoreType.DMA((STAGES * 2 * CHUNKS,)),
            pltpu.SemaphoreType.DMA((STAGES * 2 * CHUNKS,)),
            pltpu.SemaphoreType.DMA((STAGES * 2,)),
            pltpu.SemaphoreType.DMA((STAGES * 2,)),
        ],
        compiler_params=pltpu.CompilerParams(
            collective_id=0, has_side_effects=True, vmem_limit_bytes=28 * 2**20
        ),
        name="advance",
    )(level_set, normal_speed)


def reinit_kernel(rows, cols, field, band, out, t_a, t_b, gain, sign, store_sem, merged):
    wide = cols // TILE
    down = rows // TILE
    lane = lax.broadcasted_iota(jnp.int32, (8, 128), 1)
    inner = jnp.where(lane == 0, 0.0, 1.0)
    slot = lax.broadcasted_iota(jnp.int32, (8, 128), 0)
    chosen = jnp.zeros((8, 128), jnp.int32)
    for d in range(down):
        for w in range(wide):
            chosen = jnp.where(slot == d * wide + w, band[d, w], chosen)

    def source(i, j, d):
        return pl.ds((d * TILE + i) * cols + j, wide, stride=TILE)

    def place(i, j):
        return pl.ds(pl.multiple_of((i * TILE + j) * 8, 8), 8)

    def gather(i, carry):
        for j in range(TILE):
            v = jnp.concatenate([field[source(i, j, d)] for d in range(down)], axis=0)
            t_a[place(i, j)] = v
            gain[place(i, j)] = (0.3 * v) * lax.rsqrt(v * v + 1.0)
            sign[place(i, j)] = jnp.where(v > 0.0, 1.0, -1.0)
        return carry

    lax.fori_loop(0, TILE, gather, 0)

    def sweep(now, later):
        zero = jnp.zeros((8, 128), jnp.float32)
        above = [zero] * TILE
        values = [now[place(0, j)] for j in range(TILE)]
        for i in range(TILE):
            next_values = [now[place(i + 1, j)] for j in range(TILE)] if i + 1 < TILE else values
            left = zero
            next_above = []
            for j in range(TILE):
                v = values[j]
                s = sign[place(i, j)]
                below = next_values[j] - v
                right = values[j + 1] - v if j + 1 < TILE else zero
                back = (v - pltpu.roll(v, 1, 1)) * inner
                total = None
                for m, q in ((above[j], below), (left, right), (back, pltpu.roll(back, 127, 1))):
                    floor = FLOOR if total is None else 0.0
                    u = jnp.maximum(jnp.maximum(s * m, -s * q), floor)
                    total = u * u if total is None else total + u * u
                later[place(i, j)] = v - gain[place(i, j)] * (total * lax.rsqrt(total) - 1.0)
                next_above.append(below)
                left = right
            above, values = next_above, next_values

    def sweeps(index, carry):
        sweep(t_a, t_b)
        sweep(t_b, t_a)
        return carry

    lax.fori_loop(0, REINIT // 2, sweeps, 0)

    def copy_out(i, d):
        at = pl.ds(pl.multiple_of((d * TILE + i) * cols, 8), cols)
        return pltpu.make_async_copy(merged.at[at], out.at[at], store_sem.at[d * TILE + i])

    def scatter(i, carry):
        for j in range(TILE):
            v = t_a[place(i, j)]
            for d in range(down):
                at = source(i, j, d)
                part = slice(d * wide, (d + 1) * wide)
                merged[at] = jnp.where(chosen[part] > 0, v[part], field[at])
        for d in range(down):
            copy_out(i, d).start()
        return carry

    lax.fori_loop(0, TILE, scatter, 0)

    def finish(i, carry):
        for d in range(down):
            copy_out(i, d).wait()
        return carry

    lax.fori_loop(0, TILE, finish, 0)


def reinitialize(field, band, rows, cols):
    cells = rows * cols
    flat = pltpu.VMEM((cells, 128), jnp.float32)
    return pl.pallas_call(
        functools.partial(reinit_kernel, rows, cols),
        out_shape=jax.ShapeDtypeStruct((cells, 128), jnp.float32),
        in_specs=[
            pl.BlockSpec(memory_space=pltpu.VMEM),
            pl.BlockSpec(memory_space=pltpu.SMEM),
        ],
        out_specs=pl.BlockSpec(memory_space=pltpu.HBM),
        scratch_shapes=[flat, flat, flat, flat, pltpu.SemaphoreType.DMA((rows,)), flat],
        compiler_params=pltpu.CompilerParams(vmem_limit_bytes=24 * 2**20),
        name="reinitialize",
    )(field, band)


def solution(mesh):
    n_gx, n_gy = mesh.shape["gx"], mesh.shape["gy"]

    def body(level_set, normal_speed, band_tiles):
        rows, cols, depth = level_set.shape
        cells = rows * cols
        field = advance(
            level_set.reshape(cells, depth), normal_speed.reshape(cells, depth),
            rows, cols, n_gx, n_gy,
        )
        return reinitialize(field, band_tiles, rows, cols).reshape(rows, cols, depth)

    return jax.shard_map(
        body,
        mesh=mesh,
        in_specs=(
            P(("groups", "gx"), "gy", None),
            P(("groups", "gx"), "gy", None),
            P(("groups", "gx"), "gy"),
        ),
        out_specs=P(("groups", "gx"), "gy", None),
        check_vma=False,
    )
```

```python
import functools

import jax
import jax.numpy as jnp
from jax import lax
from jax.experimental import pallas as pl
from jax.experimental.pallas import tpu as pltpu
from jax.sharding import PartitionSpec as P

TILE = 16
RK_STEPS = 2
REINIT = 12
STAGES = 2 * RK_STEPS
GHOST = 3
SCALE = 1.5 ** 0.5
STEP = 0.125
EPS = 0.375e-6
TINY = 1e-37
FLOOR = 1e-18
PITCH = 140
OUT_PITCH = 132
ZPAD = 4
GAP = 8
Z_STEPS = 64
CHUNKS = 4
MESH = pl.DeviceIdType.MESH


def rcp(x):
    return pl.reciprocal(x, approx=True)


def root(x):
    return x * lax.rsqrt(jnp.maximum(x, TINY))


def stencil(e, f, half_x, half_y):
    mid = e * f + (half_x * half_y + EPS)
    rl = rcp(mid + half_y * e)
    rr = rcp(mid - half_x * e)
    rm = rcp(mid)
    return rl * rl, (rm * rm) * 6.0, rr * rr


def push(state, phi):
    last_phi, last_d, last_pair, older_pair, last_g, last_half, last_f, delta, a, left, b = state
    d = phi - last_phi
    g = d - last_d
    pair = d + last_d
    half = g * 0.5
    e = g - last_g
    f = e * (1.0 / 3.0)
    next_delta = last_f - f
    next_left, next_mid, w = stencil(e, f, last_half, half)
    aa = a * delta
    ww = w * next_delta
    both = aa + ww
    both = both + both
    weights = a + b + w
    behind = (last_pair - last_f) + (both + ww) * rcp(weights + (w + w))
    ahead = (both + aa) * rcp(weights + (a + a)) - (older_pair - last_f)
    state = (phi, d, pair, last_pair, g, half, f, next_delta, left, next_left, next_mid)
    return state, behind, ahead


def begin(cells):
    p0, p1, p2, p3, p4 = cells
    d1, d2, d3, d4 = p1 - p0, p2 - p1, p3 - p2, p4 - p3
    g1, g2, g3 = d2 - d1, d3 - d2, d4 - d3
    h1, h2, h3 = g1 * 0.5, g2 * 0.5, g3 * 0.5
    e1, e2 = g2 - g1, g3 - g2
    f1, f2 = e1 * (1.0 / 3.0), e2 * (1.0 / 3.0)
    left_a, _, _ = stencil(e1, f1, h1, h2)
    left_b, mid_b, _ = stencil(e2, f2, h2, h3)
    return (p4, d4, d4 + d3, d3 + d2, g3, h3, f2, f1 - f2, left_a, left_b, mid_b)


def upwind(sign, behind, ahead):
    v = jnp.maximum(jnp.maximum(sign * behind, sign * ahead), 0.0)
    return v * v


def by_tile(x, y, cols):
    i, j = lax.rem(x, TILE), lax.rem(y, TILE)
    slot = (x // TILE) * (cols // TILE) + y // TILE
    return pl.ds((i * TILE + j) * 8 + slot, 8, stride=8)


def advance_kernel(
    rows, cols, n_gx, n_gy,
    level, speed, out_ref,
    field_a, field_b, kept, rate, sign, acc_y, acc_z, zin, zout, zsign,
    xface, xhalo, yface, yhalo, x_send, x_recv, y_send, y_recv,
):
    cells = rows * cols
    pitch = cols + GAP
    blocks = cells // 128
    block_rows = 128 // cols
    groups = blocks // 8
    face = GHOST * rows
    slab = cols // CHUNKS
    xface_rows = GHOST * slab
    gx = lax.axis_index("gx")
    gy = lax.axis_index("gy")
    low_x, high_x = gx > 0, gx < n_gx - 1
    low_y, high_y = gy > 0, gy < n_gy - 1
    sides = (
        (low_x, {"gx": gx - 1}), (high_x, {"gx": gx + 1}),
        (low_y, {"gy": gy - 1}), (high_y, {"gy": gy + 1}),
    )

    barrier = pltpu.get_barrier_semaphore()
    for there, device in sides:
        @pl.when(there)
        def _():
            pl.semaphore_signal(barrier, inc=1, device_id=device, device_id_type=MESH)

    gap = jnp.zeros((GAP, 128), jnp.float32)
    x_zero = jnp.zeros((CHUNKS * xface_rows, 128), jnp.float32)
    y_zero = jnp.zeros((face, 128), jnp.float32)
    for stage in range(STAGES):
        for side, (there, _) in enumerate(sides[:2]):
            @pl.when(jnp.logical_not(there))
            def _(at=(stage * 2 + side) * CHUNKS * xface_rows):
                xhalo[pl.ds(at, CHUNKS * xface_rows)] = x_zero

        for side, (there, _) in enumerate(sides[2:]):
            @pl.when(jnp.logical_not(there))
            def _(at=(stage * 2 + side) * face):
                yhalo[pl.ds(at, face)] = y_zero

    for q in range(groups):
        for block in range(8):
            at = block * PITCH
            zin[q][pl.ds(at, ZPAD)] = gap[:ZPAD]
            zin[q][pl.ds(at + ZPAD + 128, PITCH - 128 - ZPAD)] = gap[: PITCH - 128 - ZPAD]

    def natural(x, y):
        return pl.ds(pl.multiple_of(x * cols + y, 8), 8)

    def spaced(x, y):
        return pl.ds(pl.multiple_of(x * pitch + y, 8), 8)

    def x_at(stage, side, chunk):
        return ((stage * 2 + side) * CHUNKS + chunk) * xface_rows

    def x_copy(stage, side, chunk):
        sem = (stage * 2 + side) * CHUNKS + chunk
        return pltpu.make_async_remote_copy(
            src_ref=xface.at[pl.ds(pl.multiple_of(x_at(stage, side, chunk), 8), xface_rows)],
            dst_ref=xhalo.at[pl.ds(pl.multiple_of(x_at(stage, 1 - side, chunk), 8), xface_rows)],
            send_sem=x_send.at[sem],
            recv_sem=x_recv.at[sem],
            device_id=sides[side][1],
            device_id_type=MESH,
        )

    def y_copy(stage, side):
        return pltpu.make_async_remote_copy(
            src_ref=yface.at[pl.ds((stage * 2 + side) * face, face)],
            dst_ref=yhalo.at[pl.ds((stage * 2 + 1 - side) * face, face)],
            send_sem=y_send.at[stage * 2 + side],
            recv_sem=y_recv.at[stage * 2 + side],
            device_id=sides[2 + side][1],
            device_id_type=MESH,
        )

    def x_start(field, stage, chunk):
        for side in range(2):
            for n in range(GHOST):
                x = n if side == 0 else rows - GHOST + n
                for y in range(0, slab, 8):
                    at = pl.multiple_of(x_at(stage, side, chunk) + n * slab + y, 8)
                    xface[pl.ds(at, 8)] = field[spaced(x, chunk * slab + y)]
        for side in range(2):
            @pl.when(sides[side][0])
            def _(side=side):
                x_copy(stage, side, chunk).start()

    def scaled(x, carry):
        field_a[pl.ds(pl.multiple_of(x * pitch, 8), cols)] = (
            level[pl.ds(pl.multiple_of(x * cols, 8), cols)] * SCALE
        )
        return carry

    lax.fori_loop(0, rows, scaled, 0, unroll=True)

    there_count = sum(there.astype(jnp.int32) for there, _ in sides)
    pl.semaphore_wait(barrier, there_count)

    def first_chunk(chunk, carry):
        x_start(field_a, 0, chunk)
        return carry

    lax.fori_loop(0, CHUNKS, first_chunk, 0)

    def signs(block, carry):
        here = pl.ds(pl.multiple_of(block * 128, 128), 128)
        v = jnp.where(speed[here] > 0.0, 1.0, -1.0)
        rate[here] = speed[here] * STEP
        for n in range(block_rows):
            at = pl.ds(pl.multiple_of((block * block_rows + n) * pitch, 8), cols)
            sign[at] = v[n * cols : (n + 1) * cols]
        return v

    for q in range(groups):
        def sign_block(block, carry):
            v = signs(q * 8 + block, carry)
            zsign[q][pl.ds(block * OUT_PITCH, 128)] = v.T
            return carry

        lax.fori_loop(0, 8, sign_block, 0, unroll=True)

    def one_stage(stage, field, fresh, write, more):
        for side in range(2):
            for n in range(GHOST):
                y = n if side == 0 else cols - GHOST + n
                for x in range(0, rows, 8):
                    yface[pl.ds((stage * 2 + side) * face + n * rows + x, 8)] = field[
                        pl.ds(x * pitch + y, 8, stride=pitch)
                    ]
        for side in range(2):
            @pl.when(sides[2 + side][0])
            def _(side=side):
                y_copy(stage, side).start()

        def flip(q, block):
            v = []
            for n in range(block_rows):
                x = (q * 8 + block) * block_rows + n
                v.append(field[pl.ds(pl.multiple_of(x * pitch, 8), cols)])
            zin[q][pl.ds(block * PITCH + ZPAD, 128)] = jnp.concatenate(v, axis=0).T

        def unflip(q, block):
            acc_z[pl.ds(pl.multiple_of((q * 8 + block) * 128, 128), 128)] = zout[q][
                pl.ds(block * OUT_PITCH, 128)
            ].T

        def flip_first(block, carry):
            flip(0, block)
            return carry

        lax.fori_loop(0, 8, flip_first, 0, unroll=True)
        trips = 128 // Z_STEPS
        for q in range(groups):
            def z_cell(z):
                return zin[q][pl.ds(ZPAD + z, 8, stride=PITCH)]

            def z_trip(trip, carry):
                def step(u, carry):
                    st, behind = carry
                    z = trip * Z_STEPS + u
                    st, next_behind, ahead = push(st, z_cell(z + 3))
                    at = pl.ds(z, 8, stride=OUT_PITCH)
                    zout[q][at] = upwind(zsign[q][at], behind, ahead)
                    return st, next_behind

                for n in range(8 // trips):
                    if q + 1 < groups:
                        flip(q + 1, trip * (8 // trips) + n)
                    if q > 0:
                        unflip(q - 1, trip * (8 // trips) + n)
                return lax.fori_loop(0, Z_STEPS, step, carry, unroll=True)

            first = push(begin([z_cell(z) for z in range(-3, 2)]), z_cell(2))
            lax.fori_loop(0, trips, z_trip, first[:2])

        for side in range(2):
            @pl.when(sides[2 + side][0])
            def _(side=side):
                y_copy(stage, 1 - side).wait_recv()

        def y_block(block, carry):
            x = block * 8

            def low_cell(n):
                return yhalo[pl.ds(pl.multiple_of((stage * 2) * face + n * rows + x, 8), 8)]

            def high_cell(n):
                return yhalo[pl.ds(pl.multiple_of((stage * 2 + 1) * face + n * rows + x, 8), 8)]

            def cell(y):
                return field[pl.ds(x * pitch + y, 8, stride=pitch)]

            def step(y, carry, phi):
                st, behind = carry
                st, next_behind, ahead = push(st, phi)
                at = pl.ds(x * pitch + y, 8, stride=pitch)
                acc_y[at] = upwind(sign[at], behind, ahead)
                return st, next_behind

            st = begin([low_cell(n) for n in range(GHOST)] + [cell(0), cell(1)])
            carried = push(st, cell(2))[:2]
            for n in range(8 // (rows // 8)):
                unflip(groups - 1, block * (8 // (rows // 8)) + n)
            carried = lax.fori_loop(
                0, cols - GHOST, lambda y, c: step(y, c, cell(y + GHOST)), carried, unroll=True
            )
            for n in range(GHOST):
                carried = step(cols - GHOST + n, carried, high_cell(n))
            return carry

        lax.fori_loop(0, rows // 8, y_block, 0)

        def x_block(chunk, y):
            def cell(x):
                return field[spaced(x, chunk * slab + y)]

            def ghost(side, n):
                at = x_at(stage, side, chunk) + n * slab + y
                return xhalo[pl.ds(pl.multiple_of(at, 8), 8)]

            def step(x, carry, phi):
                st, behind = carry
                st, next_behind, ahead = push(st, phi)
                at, here = spaced(x, chunk * slab + y), natural(x, chunk * slab + y)
                total = upwind(sign[at], behind, ahead) + (acc_y[at] + acc_z[here])
                now = cell(x)
                write(
                    now, now - rate[here] * root(total), at, here,
                    by_tile(x, chunk * slab + y, cols),
                )
                return st, next_behind

            st = begin([ghost(0, n) for n in range(GHOST)] + [cell(0), cell(1)])
            carried = push(st, cell(2))[:2]
            carried = lax.fori_loop(
                0, rows - GHOST, lambda x, c: step(x, c, cell(x + GHOST)), carried, unroll=True
            )
            for n in range(GHOST):
                carried = step(rows - GHOST + n, carried, ghost(1, n))

        def x_chunk(chunk, carry):
            for side in range(2):
                @pl.when(sides[side][0])
                def _(side=side):
                    x_copy(stage, 1 - side, chunk).wait_recv()
            for y in range(0, slab, 8):
                x_block(chunk, y)

            @pl.when(more)
            def _():
                x_start(fresh, stage + 1, chunk)
            return carry

        lax.fori_loop(0, CHUNKS, x_chunk, 0)

    def time_step(step, carry):
        last = jnp.where(step == RK_STEPS - 1, jnp.float32(0.5 / SCALE), jnp.float32(0.5))

        def halfway(now, moved, at, here, tiled):
            field_b[at] = moved
            kept[here] = now

        def whole(now, moved, at, here, tiled):
            result = last * (kept[here] + moved)
            field_a[at] = result
            out_ref[tiled] = result

        one_stage(2 * step, field_a, field_b, halfway, True)
        one_stage(2 * step + 1, field_b, field_a, whole, step < RK_STEPS - 1)
        return carry

    lax.fori_loop(0, RK_STEPS, time_step, 0)

    def sent(stage, carry):
        for side in range(2):
            @pl.when(sides[side][0])
            def _(side=side):
                for chunk in range(CHUNKS):
                    x_copy(stage, side, chunk).wait_send()

            @pl.when(sides[2 + side][0])
            def _(side=side):
                y_copy(stage, side).wait_send()
        return carry

    lax.fori_loop(0, STAGES, sent, 0)


def advance(level_set, normal_speed, rows, cols, n_gx, n_gy):
    cells = rows * cols
    groups = cells // 1024
    pitch = cols + GAP
    flat = pltpu.VMEM((cells, 128), jnp.float32)
    spaced = pltpu.VMEM((rows * pitch, 128), jnp.float32)
    return pl.pallas_call(
        functools.partial(advance_kernel, rows, cols, n_gx, n_gy),
        out_shape=jax.ShapeDtypeStruct((cells, 128), jnp.float32),
        in_specs=[pl.BlockSpec(memory_space=pltpu.VMEM)] * 2,
        out_specs=pl.BlockSpec(memory_space=pltpu.VMEM),
        scratch_shapes=[
            spaced, spaced, flat, flat, spaced, spaced, flat,
            [pltpu.VMEM((8 * PITCH, 128), jnp.float32)] * groups,
            [pltpu.VMEM((8 * OUT_PITCH, 128), jnp.float32)] * groups,
            [pltpu.VMEM((8 * OUT_PITCH, 128), jnp.float32)] * groups,
            pltpu.VMEM((STAGES * 2 * GHOST * cols, 128), jnp.float32),
            pltpu.VMEM((STAGES * 2 * GHOST * cols, 128), jnp.float32),
            pltpu.VMEM((STAGES * 2 * GHOST * rows, 128), jnp.float32),
            pltpu.VMEM((STAGES * 2 * GHOST * rows, 128), jnp.float32),
            pltpu.SemaphoreType.DMA((STAGES * 2 * CHUNKS,)),
            pltpu.SemaphoreType.DMA((STAGES * 2 * CHUNKS,)),
            pltpu.SemaphoreType.DMA((STAGES * 2,)),
            pltpu.SemaphoreType.DMA((STAGES * 2,)),
        ],
        compiler_params=pltpu.CompilerParams(
            collective_id=0, has_side_effects=True, vmem_limit_bytes=28 * 2**20
        ),
        name="advance",
    )(level_set, normal_speed)


def reinit_kernel(rows, cols, start, band, out, t_a, t_b, gain, sign, store_sem, merged):
    wide = cols // TILE
    down = rows // TILE
    lane = lax.broadcasted_iota(jnp.int32, (8, 128), 1)
    inner = jnp.where(lane == 0, 0.0, 1.0)
    slot = lax.broadcasted_iota(jnp.int32, (8, 128), 0)
    chosen = jnp.zeros((8, 128), jnp.int32)
    for d in range(down):
        for w in range(wide):
            chosen = jnp.where(slot == d * wide + w, band[d, w], chosen)

    def place(i, j):
        return pl.ds(pl.multiple_of((i * TILE + j) * 8, 8), 8)

    def gather(i, carry):
        for j in range(TILE):
            v = start[place(i, j)]
            gain[place(i, j)] = jnp.where(chosen > 0, (0.3 * v) * lax.rsqrt(v * v + 1.0), 0.0)
            sign[place(i, j)] = jnp.where(v > 0.0, 1.0, -1.0)
        return carry

    lax.fori_loop(0, TILE, gather, 0, unroll=2)

    def sweep(now, later):
        zero = jnp.zeros((8, 128), jnp.float32)
        above = [zero] * TILE
        values = [now[place(0, j)] for j in range(TILE)]
        for i in range(TILE):
            next_values = [now[place(i + 1, j)] for j in range(TILE)] if i + 1 < TILE else values
            left = zero
            next_above = []
            for j in range(TILE):
                v = values[j]
                s = sign[place(i, j)]
                below = next_values[j] - v
                right = values[j + 1] - v if j + 1 < TILE else zero
                back = (v - pltpu.roll(v, 1, 1)) * inner
                total = None
                for m, q in ((above[j], below), (left, right), (back, pltpu.roll(back, 127, 1))):
                    floor = FLOOR if total is None else 0.0
                    u = jnp.maximum(jnp.maximum(s * m, -s * q), floor)
                    total = u * u if total is None else total + u * u
                later[place(i, j)] = v - gain[place(i, j)] * (total * lax.rsqrt(total) - 1.0)
                next_above.append(below)
                left = right
            above, values = next_above, next_values

    def sweeps(index, carry):
        sweep(t_a, t_b)
        sweep(t_b, t_a)
        return carry

    sweep(start, t_b)
    sweep(t_b, t_a)
    lax.fori_loop(0, REINIT // 2 - 1, sweeps, 0)

    def copy_out(i, d):
        at = pl.ds(pl.multiple_of((d * TILE + i) * cols, 8), cols)
        return pltpu.make_async_copy(merged.at[at], out.at[at], store_sem.at[d * TILE + i])

    def scatter(i, carry):
        for d in range(down):
            for y in range(0, cols, 8):
                at = pl.ds(pl.multiple_of((d * TILE + i) * cols + y, 8), 8)
                merged[at] = t_a[by_tile(d * TILE + i, y, cols)]
        for d in range(down):
            copy_out(i, d).start()
        return carry

    lax.fori_loop(0, TILE, scatter, 0)

    def finish(i, carry):
        for d in range(down):
            copy_out(i, d).wait()
        return carry

    lax.fori_loop(0, TILE, finish, 0)


def reinitialize(field, band, rows, cols):
    cells = rows * cols
    flat = pltpu.VMEM((cells, 128), jnp.float32)
    return pl.pallas_call(
        functools.partial(reinit_kernel, rows, cols),
        out_shape=jax.ShapeDtypeStruct((cells, 128), jnp.float32),
        in_specs=[
            pl.BlockSpec(memory_space=pltpu.VMEM),
            pl.BlockSpec(memory_space=pltpu.SMEM),
        ],
        out_specs=pl.BlockSpec(memory_space=pltpu.HBM),
        scratch_shapes=[flat, flat, flat, flat, pltpu.SemaphoreType.DMA((rows,)), flat],
        compiler_params=pltpu.CompilerParams(vmem_limit_bytes=24 * 2**20),
        name="reinitialize",
    )(field, band)


def solution(mesh):
    n_gx, n_gy = mesh.shape["gx"], mesh.shape["gy"]

    def body(level_set, normal_speed, band_tiles):
        rows, cols, depth = level_set.shape
        cells = rows * cols
        field = advance(
            level_set.reshape(cells, depth), normal_speed.reshape(cells, depth),
            rows, cols, n_gx, n_gy,
        )
        return reinitialize(field, band_tiles, rows, cols).reshape(rows, cols, depth)

    return jax.shard_map(
        body,
        mesh=mesh,
        in_specs=(
            P(("groups", "gx"), "gy", None),
            P(("groups", "gx"), "gy", None),
            P(("groups", "gx"), "gy"),
        ),
        out_specs=P(("groups", "gx"), "gy", None),
        check_vma=False,
    )
```

```python
import functools

import jax
import jax.numpy as jnp
from jax import lax
from jax.experimental import pallas as pl
from jax.experimental.pallas import tpu as pltpu
from jax.sharding import PartitionSpec as P

TILE = 16
RK_STEPS = 2
REINIT = 12
STAGES = 2 * RK_STEPS
GHOST = 3
SCALE = 1.5 ** 0.5
STEP = 0.125
EPS = 0.375e-6
TINY = 1e-37
FLOOR = 1e-18
PITCH = 140
OUT_PITCH = 132
ZPAD = 4
GAP = 8
Z_STEPS = 64
CHUNKS = 4
MESH = pl.DeviceIdType.MESH


def rcp(x):
    return pl.reciprocal(x, approx=True)


def root(x):
    return x * lax.rsqrt(jnp.maximum(x, TINY))


def stencil(e, f, half_x, half_y):
    mid = e * f + (half_x * half_y + EPS)
    rl = rcp(mid + half_y * e)
    rr = rcp(mid - half_x * e)
    rm = rcp(mid)
    return rl * rl, (rm * rm) * 6.0, rr * rr


def push(state, phi):
    last_phi, last_d, last_pair, older_pair, last_g, last_half, last_f, delta, a, left, b = state
    d = phi - last_phi
    g = d - last_d
    pair = d + last_d
    half = g * 0.5
    e = g - last_g
    f = e * (1.0 / 3.0)
    next_delta = last_f - f
    next_left, next_mid, w = stencil(e, f, last_half, half)
    aa = a * delta
    ww = w * next_delta
    both = aa + ww
    both = both + both
    weights = a + b + w
    behind = (last_pair - last_f) + (both + ww) * rcp(weights + (w + w))
    ahead = (both + aa) * rcp(weights + (a + a)) - (older_pair - last_f)
    state = (phi, d, pair, last_pair, g, half, f, next_delta, left, next_left, next_mid)
    return state, behind, ahead


def begin(cells):
    p0, p1, p2, p3, p4 = cells
    d1, d2, d3, d4 = p1 - p0, p2 - p1, p3 - p2, p4 - p3
    g1, g2, g3 = d2 - d1, d3 - d2, d4 - d3
    h1, h2, h3 = g1 * 0.5, g2 * 0.5, g3 * 0.5
    e1, e2 = g2 - g1, g3 - g2
    f1, f2 = e1 * (1.0 / 3.0), e2 * (1.0 / 3.0)
    left_a, _, _ = stencil(e1, f1, h1, h2)
    left_b, mid_b, _ = stencil(e2, f2, h2, h3)
    return (p4, d4, d4 + d3, d3 + d2, g3, h3, f2, f1 - f2, left_a, left_b, mid_b)


def upwind(sign, behind, ahead):
    v = jnp.maximum(jnp.maximum(sign * behind, sign * ahead), 0.0)
    return v * v


def by_tile(x, y, cols):
    i, j = lax.rem(x, TILE), lax.rem(y, TILE)
    slot = (x // TILE) * (cols // TILE) + y // TILE
    return pl.ds((i * TILE + j) * 8 + slot, 8, stride=8)


def advance_kernel(
    rows, cols, n_gx, n_gy,
    level, speed, out_ref,
    field_a, field_b, kept, rate, sign, acc_y, acc_z, zin, zout, zsign,
    xface, xhalo, yface, yhalo, x_send, x_recv, y_send, y_recv,
):
    cells = rows * cols
    pitch = cols + GAP
    blocks = cells // 128
    block_rows = 128 // cols
    groups = blocks // 8
    face = GHOST * rows
    slab = cols // CHUNKS
    xface_rows = GHOST * slab
    gx = lax.axis_index("gx")
    gy = lax.axis_index("gy")
    low_x, high_x = gx > 0, gx < n_gx - 1
    low_y, high_y = gy > 0, gy < n_gy - 1
    sides = (
        (low_x, {"gx": gx - 1}), (high_x, {"gx": gx + 1}),
        (low_y, {"gy": gy - 1}), (high_y, {"gy": gy + 1}),
    )

    barrier = pltpu.get_barrier_semaphore()
    for there, device in sides:
        @pl.when(there)
        def _():
            pl.semaphore_signal(barrier, inc=1, device_id=device, device_id_type=MESH)

    gap = jnp.zeros((GAP, 128), jnp.float32)
    x_zero = jnp.zeros((CHUNKS * xface_rows, 128), jnp.float32)
    y_zero = jnp.zeros((face, 128), jnp.float32)
    for stage in range(STAGES):
        for side, (there, _) in enumerate(sides[:2]):
            @pl.when(jnp.logical_not(there))
            def _(at=(stage * 2 + side) * CHUNKS * xface_rows):
                xhalo[pl.ds(at, CHUNKS * xface_rows)] = x_zero

        for side, (there, _) in enumerate(sides[2:]):
            @pl.when(jnp.logical_not(there))
            def _(at=(stage * 2 + side) * face):
                yhalo[pl.ds(at, face)] = y_zero

    for q in range(groups):
        for block in range(8):
            at = block * PITCH
            zin[q][pl.ds(at, ZPAD)] = gap[:ZPAD]
            zin[q][pl.ds(at + ZPAD + 128, PITCH - 128 - ZPAD)] = gap[: PITCH - 128 - ZPAD]

    def natural(x, y):
        return pl.ds(pl.multiple_of(x * cols + y, 8), 8)

    def spaced(x, y):
        return pl.ds(pl.multiple_of(x * pitch + y, 8), 8)

    def x_at(stage, side, chunk):
        return ((stage * 2 + side) * CHUNKS + chunk) * xface_rows

    def x_copy(stage, side, chunk):
        sem = (stage * 2 + side) * CHUNKS + chunk
        return pltpu.make_async_remote_copy(
            src_ref=xface.at[pl.ds(pl.multiple_of(x_at(stage, side, chunk), 8), xface_rows)],
            dst_ref=xhalo.at[pl.ds(pl.multiple_of(x_at(stage, 1 - side, chunk), 8), xface_rows)],
            send_sem=x_send.at[sem],
            recv_sem=x_recv.at[sem],
            device_id=sides[side][1],
            device_id_type=MESH,
        )

    def y_copy(stage, side):
        return pltpu.make_async_remote_copy(
            src_ref=yface.at[pl.ds((stage * 2 + side) * face, face)],
            dst_ref=yhalo.at[pl.ds((stage * 2 + 1 - side) * face, face)],
            send_sem=y_send.at[stage * 2 + side],
            recv_sem=y_recv.at[stage * 2 + side],
            device_id=sides[2 + side][1],
            device_id_type=MESH,
        )

    def x_start(field, stage, chunk):
        for side in range(2):
            for n in range(GHOST):
                x = n if side == 0 else rows - GHOST + n
                for y in range(0, slab, 8):
                    at = pl.multiple_of(x_at(stage, side, chunk) + n * slab + y, 8)
                    xface[pl.ds(at, 8)] = field[spaced(x, chunk * slab + y)]
        for side in range(2):
            @pl.when(sides[side][0])
            def _(side=side):
                x_copy(stage, side, chunk).start()

    def scaled(x, carry):
        field_a[pl.ds(pl.multiple_of(x * pitch, 8), cols)] = (
            level[pl.ds(pl.multiple_of(x * cols, 8), cols)] * SCALE
        )
        return carry

    lax.fori_loop(0, rows, scaled, 0, unroll=True)

    there_count = sum(there.astype(jnp.int32) for there, _ in sides)
    pl.semaphore_wait(barrier, there_count)

    def first_chunk(chunk, carry):
        x_start(field_a, 0, chunk)
        return carry

    lax.fori_loop(0, CHUNKS, first_chunk, 0)

    def signs(block, carry):
        here = pl.ds(pl.multiple_of(block * 128, 128), 128)
        v = jnp.where(speed[here] > 0.0, 1.0, -1.0)
        rate[here] = speed[here] * STEP
        for n in range(block_rows):
            at = pl.ds(pl.multiple_of((block * block_rows + n) * pitch, 8), cols)
            sign[at] = v[n * cols : (n + 1) * cols]
        return v

    for q in range(groups):
        def sign_block(block, carry):
            v = signs(q * 8 + block, carry)
            zsign[q][pl.ds(block * OUT_PITCH, 128)] = v.T
            return carry

        lax.fori_loop(0, 8, sign_block, 0, unroll=True)

    def one_stage(stage, field, fresh, write, more):
        for side in range(2):
            for n in range(GHOST):
                y = n if side == 0 else cols - GHOST + n
                for x in range(0, rows, 8):
                    yface[pl.ds((stage * 2 + side) * face + n * rows + x, 8)] = field[
                        pl.ds(x * pitch + y, 8, stride=pitch)
                    ]
        for side in range(2):
            @pl.when(sides[2 + side][0])
            def _(side=side):
                y_copy(stage, side).start()

        def flip(q, block):
            v = []
            for n in range(block_rows):
                x = (q * 8 + block) * block_rows + n
                v.append(field[pl.ds(pl.multiple_of(x * pitch, 8), cols)])
            zin[q][pl.ds(block * PITCH + ZPAD, 128)] = jnp.concatenate(v, axis=0).T

        def unflip(q, block):
            acc_z[pl.ds(pl.multiple_of((q * 8 + block) * 128, 128), 128)] = zout[q][
                pl.ds(block * OUT_PITCH, 128)
            ].T

        def flip_first(block, carry):
            flip(0, block)
            return carry

        lax.fori_loop(0, 8, flip_first, 0, unroll=True)
        trips = 128 // Z_STEPS
        for q in range(groups):
            def z_cell(z):
                return zin[q][pl.ds(ZPAD + z, 8, stride=PITCH)]

            def z_trip(trip, carry):
                def step(u, carry):
                    st, behind = carry
                    z = trip * Z_STEPS + u
                    st, next_behind, ahead = push(st, z_cell(z + 3))
                    at = pl.ds(z, 8, stride=OUT_PITCH)
                    zout[q][at] = upwind(zsign[q][at], behind, ahead)
                    return st, next_behind

                for n in range(8 // trips):
                    if q + 1 < groups:
                        flip(q + 1, trip * (8 // trips) + n)
                    if q > 0:
                        unflip(q - 1, trip * (8 // trips) + n)
                return lax.fori_loop(0, Z_STEPS, step, carry, unroll=True)

            first = push(begin([z_cell(z) for z in range(-3, 2)]), z_cell(2))
            lax.fori_loop(0, trips, z_trip, first[:2])

        for side in range(2):
            @pl.when(sides[2 + side][0])
            def _(side=side):
                y_copy(stage, 1 - side).wait_recv()

        def y_block(block, carry):
            x = block * 8

            def low_cell(n):
                return yhalo[pl.ds(pl.multiple_of((stage * 2) * face + n * rows + x, 8), 8)]

            def high_cell(n):
                return yhalo[pl.ds(pl.multiple_of((stage * 2 + 1) * face + n * rows + x, 8), 8)]

            def cell(y):
                return field[pl.ds(x * pitch + y, 8, stride=pitch)]

            def step(y, carry, phi):
                st, behind = carry
                st, next_behind, ahead = push(st, phi)
                at = pl.ds(x * pitch + y, 8, stride=pitch)
                acc_y[at] = upwind(sign[at], behind, ahead)
                return st, next_behind

            st = begin([low_cell(n) for n in range(GHOST)] + [cell(0), cell(1)])
            carried = push(st, cell(2))[:2]
            for n in range(8 // (rows // 8)):
                unflip(groups - 1, block * (8 // (rows // 8)) + n)
            carried = lax.fori_loop(
                0, cols - GHOST, lambda y, c: step(y, c, cell(y + GHOST)), carried, unroll=True
            )
            for n in range(GHOST):
                carried = step(cols - GHOST + n, carried, high_cell(n))
            return carry

        lax.fori_loop(0, rows // 8, y_block, 0)

        def x_block(chunk, y):
            def cell(x):
                return field[spaced(x, chunk * slab + y)]

            def ghost(side, n):
                at = x_at(stage, side, chunk) + n * slab + y
                return xhalo[pl.ds(pl.multiple_of(at, 8), 8)]

            def step(x, carry, phi):
                st, behind = carry
                st, next_behind, ahead = push(st, phi)
                at, here = spaced(x, chunk * slab + y), natural(x, chunk * slab + y)
                total = upwind(sign[at], behind, ahead) + (acc_y[at] + acc_z[here])
                now = cell(x)
                write(
                    now, now - rate[here] * root(total), at, here,
                    by_tile(x, chunk * slab + y, cols),
                )
                return st, next_behind

            st = begin([ghost(0, n) for n in range(GHOST)] + [cell(0), cell(1)])
            carried = push(st, cell(2))[:2]
            carried = lax.fori_loop(
                0, rows - GHOST, lambda x, c: step(x, c, cell(x + GHOST)), carried, unroll=True
            )
            for n in range(GHOST):
                carried = step(rows - GHOST + n, carried, ghost(1, n))

        def x_chunk(chunk, carry):
            for side in range(2):
                @pl.when(sides[side][0])
                def _(side=side):
                    x_copy(stage, 1 - side, chunk).wait_recv()
            for y in range(0, slab, 8):
                x_block(chunk, y)

            @pl.when(more)
            def _():
                x_start(fresh, stage + 1, chunk)
            return carry

        lax.fori_loop(0, CHUNKS, x_chunk, 0)

    def time_step(step, carry):
        last = jnp.where(step == RK_STEPS - 1, jnp.float32(0.5 / SCALE), jnp.float32(0.5))

        def halfway(now, moved, at, here, tiled):
            field_b[at] = moved
            kept[here] = now

        def whole(now, moved, at, here, tiled):
            result = last * (kept[here] + moved)
            field_a[at] = result
            out_ref[tiled] = result

        one_stage(2 * step, field_a, field_b, halfway, True)
        one_stage(2 * step + 1, field_b, field_a, whole, step < RK_STEPS - 1)
        return carry

    lax.fori_loop(0, RK_STEPS, time_step, 0)

    def sent(stage, carry):
        for side in range(2):
            @pl.when(sides[side][0])
            def _(side=side):
                for chunk in range(CHUNKS):
                    x_copy(stage, side, chunk).wait_send()

            @pl.when(sides[2 + side][0])
            def _(side=side):
                y_copy(stage, side).wait_send()
        return carry

    lax.fori_loop(0, STAGES, sent, 0)


def advance(level_set, normal_speed, rows, cols, n_gx, n_gy):
    cells = rows * cols
    groups = cells // 1024
    pitch = cols + GAP
    flat = pltpu.VMEM((cells, 128), jnp.float32)
    spaced = pltpu.VMEM((rows * pitch, 128), jnp.float32)
    return pl.pallas_call(
        functools.partial(advance_kernel, rows, cols, n_gx, n_gy),
        out_shape=jax.ShapeDtypeStruct((cells, 128), jnp.float32),
        in_specs=[pl.BlockSpec(memory_space=pltpu.VMEM)] * 2,
        out_specs=pl.BlockSpec(memory_space=pltpu.VMEM),
        scratch_shapes=[
            spaced, spaced, flat, flat, spaced, spaced, flat,
            [pltpu.VMEM((8 * PITCH, 128), jnp.float32)] * groups,
            [pltpu.VMEM((8 * OUT_PITCH, 128), jnp.float32)] * groups,
            [pltpu.VMEM((8 * OUT_PITCH, 128), jnp.float32)] * groups,
            pltpu.VMEM((STAGES * 2 * GHOST * cols, 128), jnp.float32),
            pltpu.VMEM((STAGES * 2 * GHOST * cols, 128), jnp.float32),
            pltpu.VMEM((STAGES * 2 * GHOST * rows, 128), jnp.float32),
            pltpu.VMEM((STAGES * 2 * GHOST * rows, 128), jnp.float32),
            pltpu.SemaphoreType.DMA((STAGES * 2 * CHUNKS,)),
            pltpu.SemaphoreType.DMA((STAGES * 2 * CHUNKS,)),
            pltpu.SemaphoreType.DMA((STAGES * 2,)),
            pltpu.SemaphoreType.DMA((STAGES * 2,)),
        ],
        compiler_params=pltpu.CompilerParams(
            collective_id=0, has_side_effects=True, vmem_limit_bytes=28 * 2**20
        ),
        name="advance",
    )(level_set, normal_speed)


def reinit_kernel(rows, cols, start, band, out, t_a, t_b, gain, sign, minus, sign_low, minus_high, store_sem, merged):
    wide = cols // TILE
    down = rows // TILE
    lane = lax.broadcasted_iota(jnp.int32, (8, 128), 1)
    not_first = lane > 0
    not_last = lane < 127
    slot = lax.broadcasted_iota(jnp.int32, (8, 128), 0)
    chosen = jnp.zeros((8, 128), jnp.int32)
    for d in range(down):
        for w in range(wide):
            chosen = jnp.where(slot == d * wide + w, band[d, w], chosen)

    def place(i, j):
        return pl.ds(pl.multiple_of((i * TILE + j) * 8, 8), 8)

    def gather(i, carry):
        for j in range(TILE):
            v = start[place(i, j)]
            gain[place(i, j)] = jnp.where(chosen > 0, (0.3 * v) * lax.rsqrt(v * v + 1.0), 0.0)
            s = jnp.where(v > 0.0, 1.0, -1.0)
            sign[place(i, j)] = s
            minus[place(i, j)] = -s
            sign_low[place(i, j)] = jnp.where(not_first, s, 0.0)
            minus_high[place(i, j)] = jnp.where(not_last, -s, 0.0)
        return carry

    lax.fori_loop(0, TILE, gather, 0, unroll=2)

    def sweep(now, later):
        zero = jnp.zeros((8, 128), jnp.float32)
        above = [zero] * TILE
        values = [now[place(0, j)] for j in range(TILE)]
        for i in range(TILE):
            next_values = [now[place(i + 1, j)] for j in range(TILE)] if i + 1 < TILE else values
            left = zero
            next_above = []
            for j in range(TILE):
                v = values[j]
                s, ns = sign[place(i, j)], minus[place(i, j)]
                below = next_values[j] - v
                right = values[j + 1] - v if j + 1 < TILE else zero
                back = v - pltpu.roll(v, 1, 1)
                ahead = pltpu.roll(back, 127, 1)
                total = None
                for sm, sq in (
                    (s * above[j], ns * below),
                    (s * left, ns * right),
                    (sign_low[place(i, j)] * back, minus_high[place(i, j)] * ahead),
                ):
                    floor = FLOOR if total is None else 0.0
                    u = jnp.maximum(jnp.maximum(sm, sq), floor)
                    total = u * u if total is None else total + u * u
                later[place(i, j)] = v - gain[place(i, j)] * (total * lax.rsqrt(total) - 1.0)
                next_above.append(below)
                left = right
            above, values = next_above, next_values

    def sweeps(index, carry):
        sweep(t_a, t_b)
        sweep(t_b, t_a)
        return carry

    sweep(start, t_b)
    sweep(t_b, t_a)
    lax.fori_loop(0, REINIT // 2 - 1, sweeps, 0)

    def copy_out(i, d):
        at = pl.ds(pl.multiple_of((d * TILE + i) * cols, 8), cols)
        return pltpu.make_async_copy(merged.at[at], out.at[at], store_sem.at[d * TILE + i])

    def scatter(i, carry):
        for d in range(down):
            for y in range(0, cols, 8):
                at = pl.ds(pl.multiple_of((d * TILE + i) * cols + y, 8), 8)
                merged[at] = t_a[by_tile(d * TILE + i, y, cols)]
        for d in range(down):
            copy_out(i, d).start()
        return carry

    lax.fori_loop(0, TILE, scatter, 0)

    def finish(i, carry):
        for d in range(down):
            copy_out(i, d).wait()
        return carry

    lax.fori_loop(0, TILE, finish, 0)


def reinitialize(field, band, rows, cols):
    cells = rows * cols
    flat = pltpu.VMEM((cells, 128), jnp.float32)
    return pl.pallas_call(
        functools.partial(reinit_kernel, rows, cols),
        out_shape=jax.ShapeDtypeStruct((cells, 128), jnp.float32),
        in_specs=[
            pl.BlockSpec(memory_space=pltpu.VMEM),
            pl.BlockSpec(memory_space=pltpu.SMEM),
        ],
        out_specs=pl.BlockSpec(memory_space=pltpu.HBM),
        scratch_shapes=[flat] * 7 + [pltpu.SemaphoreType.DMA((rows,)), flat],
        compiler_params=pltpu.CompilerParams(vmem_limit_bytes=24 * 2**20),
        name="reinitialize",
    )(field, band)


def solution(mesh):
    n_gx, n_gy = mesh.shape["gx"], mesh.shape["gy"]

    def body(level_set, normal_speed, band_tiles):
        rows, cols, depth = level_set.shape
        cells = rows * cols
        field = advance(
            level_set.reshape(cells, depth), normal_speed.reshape(cells, depth),
            rows, cols, n_gx, n_gy,
        )
        return reinitialize(field, band_tiles, rows, cols).reshape(rows, cols, depth)

    return jax.shard_map(
        body,
        mesh=mesh,
        in_specs=(
            P(("groups", "gx"), "gy", None),
            P(("groups", "gx"), "gy", None),
            P(("groups", "gx"), "gy"),
        ),
        out_specs=P(("groups", "gx"), "gy", None),
        check_vma=False,
    )
```
